32 devices in a mesh: frames: 16 (over z, x, core), heads: 2 (over y).
Axes of the slice: x: 2, y: 2, z: 4, core: 2. Of those that a mesh axis runs over, the one named last changes fastest.
Arguments:
- query_states: bfloat16 [24576, 1024], P('frames', 'heads'), may hold values from -9 to 9
- key_states: bfloat16 [24576, 1024], P('frames', 'heads'), may hold values from -9 to 9
- value_states: bfloat16 [24576, 1024], P('frames', 'heads'), may hold values from -6 to 6
- pair_list: int32 [1024, 2], replicated, may hold values from 0 to 127, as said below
- out_weight: bfloat16 [1024, 1024], P('heads'), may hold values from -0.1875 to 0.1875
Outputs:
- attended: bfloat16 [24576, 1024], P('frames', 'heads')
The draws below stay inside these ranges and needn't reach their ends.
Inputs may be any that keep to these rules, and one draw needn't show every extreme that they name: `pair_list`: row r belongs to device r // 64 of frames: its first frame is held by that device (frames f * 8 to f * 8 + 7 on device f), its second frame j lies on device j // 8. Among the 64 rows of one device at most 4 have their second frame on any one device, and some device is reached exactly 4 times. The two frames of a row differ.
All inputs are finite; a program needn't handle non-finite values.
Results may differ from the reference program's by a relative error of at most 0.017.
Values may be sent and summed in bfloat16 or wider, within the bound.
No kernel may reach another device: no remote copies, remote signals or barrier semaphores. Data moves between devices by JAX's collectives and lax.ppermute only.
A program may use at most 192 MiB of HBM per device.

```python
import math
import jax
import jax.numpy as jnp
from jax import lax

D = 1024
HEADS = 16
HDIM = 64
TOKF = 192
FR_DEV = 8
PAIR_DEV = 64
CAP = 4
FRAMES = 128
PAIRS = 1024
ROWS = 24576
N_HEADS = 2


def draw_query_states(key, part):
    key = jax.random.fold_in(key, 1)
    noises = jnp.clip(jax.random.normal(key, (FRAMES, TOKF, D), jnp.float32), -6.0, 6.0)
    result = 1.5 * noises
    return result.reshape(FRAMES * TOKF, D).astype(jnp.bfloat16)


def draw_key_states(key, part):
    key = jax.random.fold_in(key, 2)
    noises = jnp.clip(jax.random.normal(key, (FRAMES, TOKF, D), jnp.float32), -6.0, 6.0)
    result = 1.5 * noises
    return result.reshape(FRAMES * TOKF, D).astype(jnp.bfloat16)


def draw_pair_list(key, part):
    key = jax.random.fold_in(key, 7)
    device_count = FRAMES // FR_DEV
    pair_rows = PAIR_DEV
    subkeys = jax.random.split(key, 4)
    shuffled = jax.vmap(lambda subkey: jax.random.permutation(subkey, device_count * CAP))(jax.random.split(subkeys[0], device_count))
    targets = shuffled[:, :pair_rows] // CAP
    owners_col = jnp.arange(device_count)[:, None]
    first_loc = jax.random.randint(subkeys[1], (device_count, pair_rows), 0, FR_DEV)
    second_loc = jnp.minimum(jax.random.randint(subkeys[2], (device_count, pair_rows), 0, FR_DEV), jax.random.randint(subkeys[3], (device_count, pair_rows), 0, FR_DEV))
    clashes = (targets == owners_col) & (second_loc == first_loc)
    second_loc = jnp.where(clashes, (second_loc + 1) % FR_DEV, second_loc)
    first_frame = owners_col * FR_DEV + first_loc
    second_frame = targets * FR_DEV + second_loc
    return jnp.stack([first_frame, second_frame], axis=-1).reshape(device_count * pair_rows, 2).astype(jnp.int32)


def steps_of(rng, extent, cuts, low, high):
    def one(dim, parts):
        heights = jax.random.uniform(jax.random.fold_in(jax.random.fold_in(rng, 6), dim), (parts,), jnp.float32, low / len(cuts), high / len(cuts))
        return jnp.repeat(jnp.exp(heights), extent[dim] // parts).reshape((-1,) + (1,) * (len(extent) - dim - 1))

    level = one(*cuts[0])
    for cut in cuts[1:]:
        level = level * one(*cut)
    return level


def scatter_about(rng, extent, spread, reach, cuts=(), kind=jnp.bfloat16):
    gain = steps_of(rng, extent, cuts, -0.22, 0.18) if cuts else 1.0
    values = jax.random.normal(rng, extent, jnp.float32) * spread * gain
    return jnp.minimum(jnp.maximum(values, -reach), reach).astype(kind)


def setup_inputs(seed: int = 0) -> dict:
    keys = jax.random.split(jax.random.key(seed), 6)
    return {
        "query_states": draw_query_states(jax.random.fold_in(keys[5], 71), 0),
        "key_states": draw_key_states(jax.random.fold_in(keys[5], 71), 0),
        "value_states": scatter_about(keys[2], (ROWS, D), 1.0, 6.0, ((0, 16), (1, 2))),
        "pair_list": draw_pair_list(jax.random.fold_in(keys[5], 71), 0),
        "out_weight": scatter_about(keys[4], (D, D), D ** -0.5, 0.1875, ((0, 2),)),
    }


def attend(query_rows, key_rows, value_rows):
    number = query_rows.shape[0]
    queries = query_rows.astype(jnp.float32).reshape(number, TOKF, HEADS, HDIM)
    keyed = key_rows.astype(jnp.float32).reshape(number, TOKF, HEADS, HDIM)
    valued = value_rows.astype(jnp.float32).reshape(number, TOKF, HEADS, HDIM)
    scores = jnp.einsum('bqhd,bkhd->bhqk', queries, keyed) * (1.0 / math.sqrt(HDIM))
    highest = lax.optimization_barrier(jnp.max(scores, axis=-1, keepdims=True))
    exponent = jnp.exp(scores - highest)
    totals = lax.optimization_barrier(jnp.sum(exponent, axis=-1, keepdims=True))
    weights = (exponent / totals).astype(jnp.bfloat16)
    output = jnp.einsum('bhqk,bkhd->bqhd', weights.astype(jnp.float32), valued).astype(jnp.bfloat16)
    return (output.reshape(number, TOKF, D), (highest + jnp.log(totals))[..., 0])

def project(merged, out_weight):
    groups = N_HEADS
    group_width = D // groups

    def advance(summed, group_id):
        merged_cols = lax.dynamic_slice_in_dim(merged, group_id * group_width, group_width, 1)
        weight_rows = lax.dynamic_slice_in_dim(out_weight, group_id * group_width, group_width, 0)
        head_term = jnp.dot(merged_cols, weight_rows, preferred_element_type=jnp.float32).astype(jnp.bfloat16)
        head_term = lax.optimization_barrier(head_term)
        return (summed + head_term.astype(jnp.float32), None)
    summed, _ = lax.scan(advance, jnp.zeros((ROWS, D), jnp.float32), jnp.arange(groups, dtype=jnp.int32))
    return summed.astype(jnp.bfloat16)

def reference(query_states, key_states, value_states, pair_list, out_weight):
    frame_query = query_states.reshape(FRAMES, TOKF, D)
    frame_key = key_states.reshape(FRAMES, TOKF, D)
    frame_value = value_states.reshape(FRAMES, TOKF, D)
    own_block = math.gcd(FRAMES, 32)

    def own_part(block_id):
        start = block_id * own_block
        return attend(lax.dynamic_slice_in_dim(frame_query, start, own_block, 0), lax.dynamic_slice_in_dim(frame_key, start, own_block, 0), lax.dynamic_slice_in_dim(frame_value, start, own_block, 0))
    self_out, self_lse = lax.map(own_part, jnp.arange(FRAMES // own_block, dtype=jnp.int32))
    self_out = self_out.reshape(FRAMES, TOKF, D)
    self_lse = self_lse.reshape(FRAMES, HEADS, TOKF)
    pair_size = math.gcd(PAIRS, 128)
    pair_blocks = pair_list.reshape(PAIRS // pair_size, pair_size, 2)

    def advance(state, pair_block):
        highest, totals, summed = state
        first_frame = pair_block[:, 0]
        second_frame = pair_block[:, 1]
        ahead_out, ahead_lse = attend(frame_query[first_frame], frame_key[second_frame], frame_value[second_frame])
        behind_out, behind_lse = attend(frame_query[second_frame], frame_key[first_frame], frame_value[first_frame])
        frame_ids = jnp.concatenate([first_frame, second_frame], axis=0)
        outputs = jnp.concatenate([ahead_out, behind_out], axis=0)
        log_sums = jnp.concatenate([ahead_lse, behind_lse], axis=0)
        block_top = jax.ops.segment_max(log_sums, frame_ids, num_segments=FRAMES)
        new_top = jnp.maximum(highest, block_top)
        factor = jnp.exp(highest - new_top)
        weight = jnp.exp(log_sums - new_top[frame_ids])
        totals = totals * factor + jax.ops.segment_sum(weight, frame_ids, num_segments=FRAMES)
        weighted = outputs.astype(jnp.float32).reshape(-1, TOKF, HEADS, HDIM) * jnp.transpose(weight, (0, 2, 1))[..., None]
        summed = summed * jnp.transpose(factor, (0, 2, 1))[..., None] + jax.ops.segment_sum(weighted, frame_ids, num_segments=FRAMES)
        return ((new_top, totals, summed), None)
    start_state = (self_lse, jnp.ones_like(self_lse), self_out.astype(jnp.float32).reshape(FRAMES, TOKF, HEADS, HDIM))
    final_state, _ = lax.scan(advance, start_state, pair_blocks)
    highest, totals, summed = final_state
    merged = (summed / jnp.transpose(totals, (0, 2, 1))[..., None]).reshape(ROWS, D).astype(jnp.bfloat16)
    return project(merged, out_weight)
```

```python
import functools

import jax
import jax.numpy as jnp
from jax import lax
from jax.experimental import pallas as pl
from jax.experimental.pallas import tpu as pltpu
from jax.sharding import PartitionSpec as P

HDIM = 64
TOKF = 192
LANES = 128
PACKED = 2 * TOKF
GROUP = 4
SHIFT = 16
DEAD = 1 << 30
UNROLL = 2
LOW, HIGH = 2.0**-60, 2.0**100
NEVER = -1e30
VMEM_LIMIT = 60 * 1024 * 1024


def table_kernel(planes, plane_size, group, frames_here, place_ref, ends_ref, table_ref):
    block = pl.program_id(0)
    plane, place = place_ref[0], place_ref[1]
    assert planes in (1, 4)
    plane_frames = plane_size * frames_here
    key_frames = group * frames_here
    query_frames = planes * frames_here
    width = table_ref.shape[2]
    tiles = ends_ref.shape[1]
    step = 2 * UNROLL

    def bits(size):
        assert size & (size - 1) == 0
        return size.bit_length() - 1

    def iota(shape, axis):
        return lax.broadcasted_iota(jnp.int32, shape, axis)

    candidates = []
    for side in range(2):
        for tile in range(tiles):
            pair = [ends_ref[end, tile : tile + 1] ^ (plane << bits(plane_frames)) for end in (side, 1 - side)]
            candidates.append((pair[0], pair[1], None))
    lane = iota((1, LANES), 1)
    chunk = lane >> bits(frames_here)
    mine = (
        ((((chunk & 1) << 1) + (((chunk >> 1) ^ chunk) & 1)) << bits(plane_frames))
        + (place << bits(frames_here))
        + (lane & (frames_here - 1))
    )
    candidates.append((mine, mine, lane < query_frames))

    lives, queries, keys, hits = [], [], [], []
    for asked, key, valid in candidates:
        live = (key >> bits(key_frames) == block) & (
            (asked >> bits(frames_here)) & (plane_size - 1) == place
        )
        if valid is not None:
            live = live & valid
        distance = asked >> bits(plane_frames)
        chunk = ((distance ^ (distance >> 1)) & 1) * 2 + (distance >> 1)
        query = (chunk << bits(frames_here)) + (asked & (frames_here - 1))
        query = jnp.where(live, query, query_frames)
        lives.append(live)
        queries.append(query)
        keys.append(key & (key_frames - 1))
        hits.append(jnp.where(query == iota((query_frames, LANES), 0), 1.0, 0.0))
    stacked = jnp.concatenate(hits, axis=0).astype(jnp.bfloat16)

    def product(left, right):
        return jnp.dot(left.astype(jnp.bfloat16), right.astype(jnp.bfloat16), preferred_element_type=jnp.float32)

    def ones_where(condition):
        return jnp.where(condition, 1.0, 0.0)

    square = (LANES, LANES)
    earlier = product(stacked, ones_where(iota(square, 0) < iota(square, 1)))
    every = product(stacked, jnp.ones(square, jnp.float32))
    before = [jnp.zeros((query_frames, LANES), jnp.float32)]
    for tile in range(len(hits)):
        before.append(before[-1] + every[tile * query_frames : (tile + 1) * query_frames])
    used = 2.0 * jnp.floor((before[-1] + 1.0) * 0.5)
    square = (query_frames, query_frames)
    row, column = iota(square, 0), iota(square, 1)
    row_chunk, column_chunk = row >> bits(frames_here), column >> bits(frames_here)
    inside = product(ones_where((row_chunk == column_chunk) & (column < row)), used)
    whole = product(ones_where(row_chunk == column_chunk), used)
    steps = jnp.floor((whole + (step - 1.0)) * (1.0 / step))
    leads = column & (frames_here - 1) == 0
    chunk_start = product(ones_where((column_chunk < row_chunk) & leads), steps)
    start = inside + step * chunk_start

    frame = iota((query_frames, LANES), 0)
    at = iota((query_frames, LANES), 1)
    first = frame & (frames_here - 1) == 0
    starts = jnp.where(first & (at == frame >> bits(frames_here)), chunk_start, 0.0)
    starts = starts + jnp.where(first & (at == planes), steps, 0.0)
    starts = jnp.sum(starts, axis=0, keepdims=True).astype(jnp.int32)

    placed, values = [], []
    for tile, hit in enumerate(hits):
        rank = earlier[tile * query_frames : (tile + 1) * query_frames] + before[tile] + start
        slot = jnp.sum(hit * rank, axis=0, keepdims=True).astype(jnp.int32)
        slot = jnp.where(lives[tile], slot, -1)
        placed.append(ones_where(slot == iota((width, LANES), 0)).astype(jnp.bfloat16))
        kind = iota((8, LANES), 0)
        value = jnp.where(kind == 0, queries[tile], jnp.where(kind == 1, keys[tile], 1))
        values.append(value.astype(jnp.float32).astype(jnp.bfloat16))
    codes = lax.dot_general(
        jnp.concatenate(values, axis=1),
        jnp.concatenate(placed, axis=1),
        (((1,), (1,)), ((), ())),
        preferred_element_type=jnp.float32,
    ).astype(jnp.int32)
    code = jnp.where(codes[2:3] > 0, (codes[0:1] << SHIFT) + codes[1:2], DEAD)
    starts = jnp.concatenate([starts] * (width // LANES), axis=1)
    table_ref[0] = jnp.where(iota((2, width), 0) == 0, code, starts)


def attend_table(pair_list, planes, plane_size, group, frames_here, places):
    peers = planes * plane_size
    rows = pair_list.shape[0]
    blocks = peers // group
    number = 2 * planes * group * (rows // peers // peers) + frames_here
    most = number + planes * frames_here + planes * (2 * UNROLL - 2)
    width = (most + LANES - 1) // LANES * LANES
    ends = pair_list.T.reshape(2, rows // LANES, LANES)
    return pl.pallas_call(
        functools.partial(table_kernel, planes, plane_size, group, frames_here),
        grid=(blocks,),
        in_specs=[
            pl.BlockSpec(memory_space=pltpu.SMEM),
            pl.BlockSpec(ends.shape, lambda block: (0, 0, 0)),
        ],
        out_specs=pl.BlockSpec((1, 2, width), lambda block: (block, 0, 0)),
        out_shape=jax.ShapeDtypeStruct((blocks, 2, width), jnp.int32),
        compiler_params=pltpu.CompilerParams(vmem_limit_bytes=VMEM_LIMIT),
    )(places, ends)


def attend_kernel(
    begin, number, chunks, sources, states, ends, table_ref, place_ref, order_ref, *refs
):
    del order_ref
    query_refs, refs = refs[: len(chunks)], refs[len(chunks) :]
    pair_refs = []
    for parts in sources:
        pair_refs.append(refs[:parts])
        refs = refs[parts:]
    state_refs, refs = refs[: 2 * states], refs[2 * states :]
    done_ref, refs = refs[0], refs[1:]
    done_ref[...] = jnp.zeros_like(done_ref)
    outs = len(chunks) if ends else 2
    out_refs, refs = refs[:outs], refs[outs:]
    sum_ref, total_ref, pair_ref, wide_ref, query_ref, score_ref, arrived, left = refs[:8]
    frames_here = query_refs[0].shape[0]
    group = pair_ref.shape[1]
    per_source = max(pair_refs[0][0].shape[0] // group, 1)
    first_frame = chunks[0] * frames_here
    query_frames = len(chunks) * frames_here
    held_from = 0 if ends else begin

    def copies(block, slot, source):
        refs_here = pair_refs[source]
        if len(refs_here) == 1:
            part = refs_here[0].at[pl.ds(block % per_source * group, group)]
            return [pltpu.make_async_copy(part, pair_ref.at[slot], arrived.at[slot])]
        result = []
        for far, ref in enumerate(refs_here):
            here = pair_ref.at[slot, pl.ds((place_ref[1] // 2 ^ far) * 2, 2)]
            result.append(pltpu.make_async_copy(ref, here, arrived.at[slot]))
        return result

    def fetch(block, slot):
        for source in range(len(sources)):

            @pl.when((block - held_from) // per_source == source)
            def _():
                for copy in copies(block, slot, source):
                    copy.start()

    def over_blocks(first_block, turns, step, ahead=None, before=None, behind=None):
        def visit(turn, carry):
            block = first_block + turn

            @pl.when(turn + 1 < turns)
            def _():
                fetch(block + 1, (turn + 1) % 2)

            whole = pair_ref.at[turn % 2]
            pltpu.make_async_copy(whole, whole, arrived.at[turn % 2]).wait()

            def units_of(index):
                first = index * 2 * UNROLL
                codes = [table_ref[block, 0, first + member] for member in range(2 * UNROLL)]
                return [codes[2 * unit : 2 * unit + 2] for unit in range(UNROLL)]

            def several(index, inner):
                step(turn % 2, units_of(index), units_of(index + 1) if ahead else None)
                return inner

            for index, chunk in enumerate(chunks):
                if before:
                    before(index)
                begins = table_ref[block, 1, chunk]
                if ahead:
                    ahead(turn % 2, units_of(begins))
                lax.fori_loop(begins, table_ref[block, 1, chunk + 1], several, 0)
                if behind:
                    behind(index)
            return carry

        if turns == 1:
            visit(0, 0)
        else:
            lax.fori_loop(0, turns, visit, 0)

    def frames_at(slot, unit):
        keys = []
        for code in unit:
            key_frame = code & ((1 << SHIFT) - 1)
            keys.append((slot, key_frame // frames_here, key_frame % frames_here))
        here = (unit[0] >> SHIFT) - first_frame
        return jnp.where((here >= 0) & (here < query_frames), here, 0), keys

    def scores_of(slot, unit):
        query_frame, keys = frames_at(slot, unit)
        held = jnp.concatenate([pair_ref[slot, device, 0, frame] for slot, device, frame in keys], axis=0)
        return lax.dot_general(
            wide_ref[query_frame], held, (((1,), (1,)), ((), ())), preferred_element_type=jnp.float32
        )

    def bias_of(unit):
        lane = lax.broadcasted_iota(jnp.int32, (1, PACKED), 1)
        bias = [jnp.where(code < DEAD, 0.0, NEVER) for code in unit]
        return jnp.where(lane < TOKF, bias[0], bias[1])

    def sums_of(keys, weights):
        held = jnp.concatenate([pair_ref[slot, device, 1, frame] for slot, device, frame in keys], axis=0)
        return by_head(
            jnp.dot(weights.astype(jnp.bfloat16), held, preferred_element_type=jnp.float32)
        )

    def by_head(both):
        lane = lax.broadcasted_iota(jnp.int32, (TOKF, LANES), 1)
        return jnp.where(lane < HDIM, both[:TOKF], both[TOKF:])

    def totals_of(weights):
        folded = weights[:, :LANES] + weights[:, LANES : 2 * LANES] + weights[:, 2 * LANES :]
        return by_head(folded + pltpu.roll(folded, HDIM, 1))

    def look_ahead(slot, units):
        for place, unit in enumerate(units):
            score_ref[place] = scores_of(slot, unit)

    def plain(slot, units, following):
        results = []
        for place, unit in enumerate(units):
            query_frame, keys = frames_at(slot, unit)
            weights = jnp.exp(score_ref[place] + bias_of(unit))
            score_ref[place] = scores_of(slot, following[place])
            results.append((query_frame, sums_of(keys, weights), totals_of(weights)))
        for query_frame, summed, total in results:
            sum_ref[query_frame] += summed
            total_ref[query_frame] += total

    asked = [
        pltpu.make_async_copy(ref, query_ref.at[index], left.at[index])
        for index, ref in enumerate(query_refs)
    ]
    for copy in asked:
        copy.start()
    fetch(begin, 0)
    frames_of = [pl.ds(index * frames_here, frames_here) for index in range(len(chunks))]
    taken, put = [], []
    for piece in range(states):
        old_refs = state_refs[2 * piece : 2 * piece + 2]
        pieces_chunks = old_refs[0].shape[0] // frames_here
        for index in range(pieces_chunks):
            if len(taken) == len(chunks):
                break
            begin_chunk = chunks[0] if states == 1 and pieces_chunks > len(chunks) else 0
            source = pl.ds((begin_chunk + index) * frames_here, frames_here)
            place = len(taken)
            taken.append(
                [
                    pltpu.make_async_copy(
                        old_ref.at[source], new_ref.at[frames_of[place]], arrived.at[2 + place]
                    )
                    for old_ref, new_ref in zip(old_refs, (sum_ref, total_ref))
                ]
            )
    for copies_here in taken:
        for copy in copies_here:
            copy.start()

    def widen(index):
        asked[index].wait()

        def one(frame, carry):
            rows = query_ref[index, frame] * jnp.asarray(HDIM**-0.5, wide_ref.dtype)
            first = lax.broadcasted_iota(jnp.int32, rows.shape, 1) < HDIM
            zeros = jnp.zeros_like(rows)
            wide_ref[index * frames_here + frame, :TOKF] = jnp.where(first, rows, zeros)
            wide_ref[index * frames_here + frame, TOKF:] = jnp.where(first, zeros, rows)
            return carry

        lax.fori_loop(0, frames_here, one, 0, unroll=4)

    def clear(frame, carry):
        sum_ref[frame] = jnp.zeros(sum_ref.shape[1:], sum_ref.dtype)
        total_ref[frame] = jnp.zeros(total_ref.shape[1:], total_ref.dtype)
        return carry

    for index in range(len(chunks)):
        widen(index)
    if not states:
        lax.fori_loop(0, query_frames, clear, 0, unroll=4)

    def enter(index):
        if states:
            for ref in (sum_ref, total_ref):
                part = ref.at[frames_of[index]]
                pltpu.make_async_copy(part, part, arrived.at[2 + index]).wait()

    def leave(index):
        if not ends:
            for ref, out in zip((sum_ref, total_ref), out_refs):
                copy = pltpu.make_async_copy(
                    ref.at[frames_of[index]], out.at[frames_of[index]], left.at[index]
                )
                copy.start()
                put.append(copy)

    if number == 1:
        over_blocks(begin, number, plain, look_ahead, enter, leave)
    else:
        for index in range(len(chunks)):
            enter(index)
        over_blocks(begin, number, plain, look_ahead)
        for index in range(len(chunks)):
            leave(index)
    for copy in put:
        copy.wait()
    if not ends:
        return
    whole_ref, top_ref = refs[8:]

    def gather_totals(frame, carry):
        total = total_ref[frame]
        square = (LANES, LANES)
        same = lax.broadcasted_iota(jnp.int32, square, 0) // HDIM == lax.broadcasted_iota(jnp.int32, square, 1) // HDIM
        ones = jnp.where(same, 1.0, 0.0).astype(jnp.bfloat16)
        high = total.astype(jnp.bfloat16)
        low = (total - high.astype(jnp.float32)).astype(jnp.bfloat16)
        whole_ref[frame] = jnp.dot(high, ones, preferred_element_type=jnp.float32) + jnp.dot(
            low, ones, preferred_element_type=jnp.float32
        )
        return carry

    lax.fori_loop(0, query_frames, gather_totals, 0, unroll=4)
    within = (jnp.min(whole_ref[...]) > LOW) & (jnp.max(whole_ref[...]) < HIGH)

    @pl.when(jnp.logical_not(within))
    def _():
        lax.fori_loop(0, query_frames, clear, 0)
        top_ref[...] = jnp.full_like(top_ref, 2 * NEVER)

        def shifted(slot, units, _):
            for unit in units:
                query_frame, keys = frames_at(slot, unit)
                scores = scores_of(slot, unit) + bias_of(unit)
                old = top_ref[query_frame]
                new = jnp.maximum(old, jnp.max(scores, axis=1, keepdims=True))
                keep = by_head(jnp.exp(old - new))
                weights = jnp.exp(scores - new[:, :1])
                sum_ref[query_frame] = sum_ref[query_frame] * keep + sums_of(keys, weights)
                total_ref[query_frame] = total_ref[query_frame] * keep + totals_of(weights)
                top_ref[query_frame] = new

        fetch(0, 0)
        over_blocks(0, len(sources) * per_source, shifted)
        lax.fori_loop(0, query_frames, gather_totals, 0)

    for index, out_ref in enumerate(out_refs):

        def finish(frame, carry):
            here = index * frames_here + frame
            out_ref[frame] = (sum_ref[here] / whole_ref[here]).astype(out_ref.dtype)
            return carry

        lax.fori_loop(0, frames_here, finish, 0, unroll=4)


def attend(queries, chunks, pairs, table, places, order, begin, number, group, state, ends):
    frames_here = queries[0].shape[0]
    shape = (len(chunks) * frames_here, TOKF, LANES)
    held = jax.ShapeDtypeStruct(shape, jnp.float32)
    whole = pl.BlockSpec(memory_space=pltpu.VMEM)
    scalars = pl.BlockSpec(memory_space=pltpu.SMEM)
    stays = pl.BlockSpec(memory_space=pltpu.HBM)
    room = pltpu.VMEM(shape, jnp.float32)
    wide = (shape[0], PACKED, LANES)
    common = [
        pltpu.VMEM((2, group) + pairs[0][0].shape[1:], queries[0].dtype),
        pltpu.VMEM(wide, queries[0].dtype),
        pltpu.VMEM((len(chunks),) + queries[0].shape, queries[0].dtype),
        pltpu.VMEM((UNROLL, PACKED, PACKED), jnp.float32),
        pltpu.SemaphoreType.DMA((2 + len(chunks),)),
        pltpu.SemaphoreType.DMA((len(chunks),)),
    ]
    listed = [array for plane in pairs for array in plane] + [array for pair in state for array in pair]
    return pl.pallas_call(
        functools.partial(
            attend_kernel,
            begin,
            number,
            tuple(chunks),
            tuple(len(plane) for plane in pairs),
            len(state),
            ends,
        ),
        in_specs=[scalars, scalars] + [stays] * (1 + len(queries) + len(listed)),
        out_specs=[whole] + ([whole] * len(chunks) if ends else [stays, stays]),
        out_shape=[jax.ShapeDtypeStruct(order.shape, order.dtype)]
        + (
            [jax.ShapeDtypeStruct(query.shape, query.dtype) for query in queries]
            if ends
            else [held, held]
        ),
        scratch_shapes=[room] * 2
        + common
        + ([room, pltpu.VMEM(wide, jnp.float32)] if ends else []),
        compiler_params=pltpu.CompilerParams(vmem_limit_bytes=VMEM_LIMIT),
        cost_estimate=pl.CostEstimate(flops=1, bytes_accessed=1, transcendentals=0),
    )(table, places, order, *queries, *listed)


def project_kernel(parts, place_ref, near_ref, far_ref, *refs):
    plane, side = place_ref[0], place_ref[2]
    out_ref = refs[2 * parts]
    columns = out_ref.shape[1]
    mine = pl.ds(pl.multiple_of(side * columns, columns), columns)
    rows = [pl.ds(pl.multiple_of((plane ^ part) * LANES, LANES), LANES) for part in range(parts)]
    merged = jnp.concatenate([ref[...] for ref in refs[: 2 * parts]], axis=1)
    weight = [near_ref[row, mine] for row in rows] + [far_ref[row, :] for row in rows]
    out_ref[...] = jnp.dot(
        merged, jnp.concatenate(weight, axis=0), preferred_element_type=jnp.float32
    ).astype(out_ref.dtype)


def project(merged, others, near, far, places):
    rows = merged[0].shape[0]
    tile = rows // 4 if rows % 64 == 0 else rows
    parts = merged + others
    columns = far.shape[1]
    return pl.pallas_call(
        functools.partial(project_kernel, len(merged)),
        grid=(rows // tile,),
        in_specs=[pl.BlockSpec(memory_space=pltpu.SMEM)]
        + [pl.BlockSpec(weight.shape, lambda row: (0, 0)) for weight in (near, far)]
        + [pl.BlockSpec((tile, part.shape[1]), lambda row: (row, 0)) for part in parts],
        out_specs=pl.BlockSpec((tile, columns), lambda row: (row, 0)),
        out_shape=jax.ShapeDtypeStruct((rows, columns), parts[0].dtype),
        compiler_params=pltpu.CompilerParams(vmem_limit_bytes=VMEM_LIMIT),
        cost_estimate=pl.CostEstimate(
            flops=4 * rows * far.size, bytes_accessed=rows * 4096, transcendentals=0
        ),
    )(places, near, far, *parts)


def spread(queries, pairs, far, table, places, swap, across, gather, plane_size):
    chunk_order = [0, 3, 1, 2]
    barrier = lax.optimization_barrier
    order = jnp.zeros((8, LANES), jnp.int32)

    def run(distances, plane, keyed, state, ends=False, number=1):
        return attend(
            [queries[distance] for distance in distances],
            [chunk_order.index(distance) for distance in distances],
            keyed if ends else keyed[plane : plane + number],
            table,
            places,
            order,
            plane,
            number,
            plane_size,
            state,
            ends,
        )

    def gathered(distance):
        return [gather(pairs[distance], plane_size)]

    keyed = [gathered(0), None, None, None]
    queries[3], queries[1] = swap(queries[3], 3), swap(queries[1], 1)
    queries[3], queries[1], pairs[1], table, order = barrier(
        (queries[3], queries[1], pairs[1], table, order)
    )
    pairs[1] = swap(pairs[1], 1)
    pairs[1], pairs[3], far, order = barrier((pairs[1], pairs[3], far, order))
    keyed[1] = gathered(1)
    pairs[3], far = swap(pairs[3], 3), across(far)
    order, *state = run([0, 3, 1], 0, keyed, [])
    pairs[3], pairs[2], far, order = barrier((pairs[3], pairs[2], far, order))
    keyed[3] = gathered(3)
    pairs[2] = swap(pairs[2], 2)
    order, *state = run([0, 3, 1], 1, keyed, [state])
    pairs[2], queries[2], order = barrier((pairs[2], queries[2], order))
    keyed[2] = gathered(2)
    queries[2] = swap(queries[2], 2)
    order, *state = run([0, 3, 1], 3, keyed, [state])
    queries[2], order = barrier((queries[2], order))
    order, *last = run([2], 0, keyed, [], number=2)
    merged, others = [None] * 4, [None] * 4

    def rows_of(out):
        return out.reshape(-1, LANES)

    order, out = run([2], 2, keyed, [last], True, 2)
    out, order = barrier((rows_of(out), order))
    merged[2] = swap(out, 2)
    order, near_out, out = run([0, 3], 2, keyed, [state], True)
    merged[0], out, merged[2], order = barrier((rows_of(near_out), rows_of(out), merged[2], order))
    merged[3], others[0], others[2] = swap(out, 3), across(merged[0]), across(merged[2])
    order, out = run([1], 2, keyed, [state], True)
    out, merged[3], others[0], others[2] = barrier((rows_of(out), merged[3], others[0], others[2]))
    merged[1], others[3] = swap(out, 1), across(merged[3])
    others[1] = across(merged[1])
    return merged, others, far


def body(query_states, key_states, value_states, pair_list, out_weight):
    peers = lax.axis_size("frames")
    my_index = lax.axis_index("frames")
    rows, columns = query_states.shape
    frames_here = rows // TOKF
    planes = columns // LANES
    plane_size = peers // planes
    group = min(plane_size, GROUP)
    plane, place = my_index // plane_size, my_index % plane_size
    side = lax.axis_index("heads")
    places = jnp.stack([plane, place, side]).astype(jnp.int32)
    table = attend_table(pair_list, planes, plane_size, group, frames_here, places)
    per_plane = plane_size // group

    def swap(array, distance, axis=plane_size):
        if distance == 0:
            return array
        return lax.ppermute(
            array, "frames", [(index, index ^ (distance * axis)) for index in range(peers)]
        )

    def gather(array, size):
        members = [list(range(start, start + size)) for start in range(0, peers, size)]
        return lax.all_gather(array, "frames", axis_index_groups=members)

    def across(array):
        return lax.ppermute(array, "heads", [(0, 1), (1, 0)])

    def columns_of(array, distance):
        chosen = lax.dynamic_slice_in_dim(array, (plane ^ distance) * LANES, LANES, 1)
        return chosen.reshape(frames_here, TOKF, LANES)

    queries = [columns_of(query_states, distance) for distance in range(planes)]
    pairs = [
        jnp.stack([columns_of(key_states, distance), columns_of(value_states, distance)])
        for distance in range(planes)
    ]
    two = lax.axis_size("heads") == 2
    far = lax.dynamic_slice_in_dim(out_weight, (1 - side) * columns, columns, 1)
    if planes == 1:
        keyed = [[gather(pairs[0], plane_size)]]
        order = jnp.zeros((8, LANES), jnp.int32)
        _, out = attend(
            queries, [0], keyed, table, places, order, 0, per_plane, group, [], True
        )
        out = out.reshape(rows, LANES)
        if not two:
            term = jnp.dot(out, out_weight, preferred_element_type=jnp.float32)
            return lax.psum_scatter(
                term.astype(out.dtype), "heads", scatter_dimension=1, tiled=True
            )
        return project([out], [across(out)], out_weight, across(far), places)
    assert two
    merged, others, far = spread(
        queries, pairs, far, table, places, swap, across, gather, plane_size
    )
    return project(merged, others, out_weight, far, places)


def solution(mesh):
    placed = (
        P("frames", "heads"),
        P("frames", "heads"),
        P("frames", "heads"),
        P(),
        P("heads", None),
    )
    return jax.shard_map(
        body, mesh=mesh, in_specs=placed, out_specs=P("frames", "heads"), check_vma=False
    )
```

```python
import functools

import jax
import jax.numpy as jnp
from jax import lax
from jax.experimental import pallas as pl
from jax.experimental.pallas import tpu as pltpu
from jax.sharding import PartitionSpec as P

HDIM = 64
TOKF = 192
LANES = 128
PACKED = 2 * TOKF
GROUP = 4
SHIFT = 16
DEAD = 1 << 30
UNROLL = 2
LOW, HIGH = 2.0**-60, 2.0**100
NEVER = -1e30
VMEM_LIMIT = 60 * 1024 * 1024


def table_kernel(planes, plane_size, group, frames_here, place_ref, ends_ref, table_ref):
    block = pl.program_id(0)
    plane, place = place_ref[0], place_ref[1]
    assert planes in (1, 4)
    plane_frames = plane_size * frames_here
    key_frames = group * frames_here
    query_frames = planes * frames_here
    width = table_ref.shape[2]
    tiles = ends_ref.shape[1]
    step = 2 * UNROLL

    def bits(size):
        assert size & (size - 1) == 0
        return size.bit_length() - 1

    def iota(shape, axis):
        return lax.broadcasted_iota(jnp.int32, shape, axis)

    candidates = []
    for side in range(2):
        for tile in range(tiles):
            pair = [ends_ref[end, tile : tile + 1] ^ (plane << bits(plane_frames)) for end in (side, 1 - side)]
            candidates.append((pair[0], pair[1], None))
    lane = iota((1, LANES), 1)
    chunk = lane >> bits(frames_here)
    mine = (
        ((((chunk & 1) << 1) + (((chunk >> 1) ^ chunk) & 1)) << bits(plane_frames))
        + (place << bits(frames_here))
        + (lane & (frames_here - 1))
    )
    candidates.append((mine, mine, lane < query_frames))

    lives, queries, keys, hits = [], [], [], []
    for asked, key, valid in candidates:
        live = (key >> bits(key_frames) == block) & (
            (asked >> bits(frames_here)) & (plane_size - 1) == place
        )
        if valid is not None:
            live = live & valid
        distance = asked >> bits(plane_frames)
        chunk = ((distance ^ (distance >> 1)) & 1) * 2 + (distance >> 1)
        query = (chunk << bits(frames_here)) + (asked & (frames_here - 1))
        query = jnp.where(live, query, query_frames)
        lives.append(live)
        queries.append(query)
        keys.append(key & (key_frames - 1))
        hits.append(jnp.where(query == iota((query_frames, LANES), 0), 1.0, 0.0))
    stacked = jnp.concatenate(hits, axis=0).astype(jnp.bfloat16)

    def product(left, right):
        return jnp.dot(left.astype(jnp.bfloat16), right.astype(jnp.bfloat16), preferred_element_type=jnp.float32)

    def ones_where(condition):
        return jnp.where(condition, 1.0, 0.0)

    square = (LANES, LANES)
    earlier = product(stacked, ones_where(iota(square, 0) < iota(square, 1)))
    every = product(stacked, jnp.ones(square, jnp.float32))
    before = [jnp.zeros((query_frames, LANES), jnp.float32)]
    for tile in range(len(hits)):
        before.append(before[-1] + every[tile * query_frames : (tile + 1) * query_frames])
    used = 2.0 * jnp.floor((before[-1] + 1.0) * 0.5)
    square = (query_frames, query_frames)
    row, column = iota(square, 0), iota(square, 1)
    row_chunk, column_chunk = row >> bits(frames_here), column >> bits(frames_here)
    inside = product(ones_where((row_chunk == column_chunk) & (column < row)), used)
    whole = product(ones_where(row_chunk == column_chunk), used)
    steps = jnp.floor((whole + (step - 1.0)) * (1.0 / step))
    leads = column & (frames_here - 1) == 0
    chunk_start = product(ones_where((column_chunk < row_chunk) & leads), steps)
    start = inside + step * chunk_start

    frame = iota((query_frames, LANES), 0)
    at = iota((query_frames, LANES), 1)
    first = frame & (frames_here - 1) == 0
    starts = jnp.where(first & (at == frame >> bits(frames_here)), chunk_start, 0.0)
    starts = starts + jnp.where(first & (at == planes), steps, 0.0)
    starts = jnp.sum(starts, axis=0, keepdims=True).astype(jnp.int32)

    placed, values = [], []
    for tile, hit in enumerate(hits):
        rank = earlier[tile * query_frames : (tile + 1) * query_frames] + before[tile] + start
        slot = jnp.sum(hit * rank, axis=0, keepdims=True).astype(jnp.int32)
        slot = jnp.where(lives[tile], slot, -1)
        placed.append(ones_where(slot == iota((width, LANES), 0)).astype(jnp.bfloat16))
        kind = iota((8, LANES), 0)
        value = jnp.where(kind == 0, queries[tile], jnp.where(kind == 1, keys[tile], 1))
        values.append(value.astype(jnp.float32).astype(jnp.bfloat16))
    codes = lax.dot_general(
        jnp.concatenate(values, axis=1),
        jnp.concatenate(placed, axis=1),
        (((1,), (1,)), ((), ())),
        preferred_element_type=jnp.float32,
    ).astype(jnp.int32)
    code = jnp.where(codes[2:3] > 0, (codes[0:1] << SHIFT) + codes[1:2], DEAD)
    starts = jnp.concatenate([starts] * (width // LANES), axis=1)
    table_ref[0] = jnp.where(iota((2, width), 0) == 0, code, starts)


def attend_table(pair_list, planes, plane_size, group, frames_here, places):
    peers = planes * plane_size
    rows = pair_list.shape[0]
    blocks = peers // group
    number = 2 * planes * group * (rows // peers // peers) + frames_here
    most = number + planes * frames_here + planes * (2 * UNROLL - 2)
    width = (most + LANES - 1) // LANES * LANES
    ends = pair_list.T.reshape(2, rows // LANES, LANES)
    return pl.pallas_call(
        functools.partial(table_kernel, planes, plane_size, group, frames_here),
        grid=(blocks,),
        in_specs=[
            pl.BlockSpec(memory_space=pltpu.SMEM),
            pl.BlockSpec(ends.shape, lambda block: (0, 0, 0)),
        ],
        out_specs=pl.BlockSpec((1, 2, width), lambda block: (block, 0, 0)),
        out_shape=jax.ShapeDtypeStruct((blocks, 2, width), jnp.int32),
        compiler_params=pltpu.CompilerParams(vmem_limit_bytes=VMEM_LIMIT),
    )(places, ends)


def attend_kernel(
    begin, number, chunks, sources, states, ends, table_ref, place_ref, order_ref, *refs
):
    del order_ref
    query_refs, refs = refs[: len(chunks)], refs[len(chunks) :]
    pair_refs = []
    for parts in sources:
        pair_refs.append(refs[:parts])
        refs = refs[parts:]
    state_refs, refs = refs[: 2 * states], refs[2 * states :]
    done_ref, refs = refs[0], refs[1:]
    done_ref[...] = jnp.zeros_like(done_ref)
    outs = len(chunks) if ends else 2
    out_refs, refs = refs[:outs], refs[outs:]
    sum_ref, total_ref, pair_ref, wide_ref, query_ref, score_ref, arrived, left = refs[:8]
    frames_here = query_refs[0].shape[0]
    group = pair_ref.shape[1]
    per_source = max(pair_refs[0][0].shape[0] // group, 1)
    first_frame = chunks[0] * frames_here
    query_frames = len(chunks) * frames_here
    held_from = 0 if ends else begin

    def copies(block, slot, source):
        refs_here = pair_refs[source]
        if len(refs_here) == 1:
            part = refs_here[0].at[pl.ds(block % per_source * group, group)]
            return [pltpu.make_async_copy(part, pair_ref.at[slot], arrived.at[slot])]
        result = []
        for far, ref in enumerate(refs_here):
            here = pair_ref.at[slot, pl.ds((place_ref[1] // 2 ^ far) * 2, 2)]
            result.append(pltpu.make_async_copy(ref, here, arrived.at[slot]))
        return result

    def fetch(block, slot):
        for source in range(len(sources)):

            @pl.when((block - held_from) // per_source == source)
            def _():
                for copy in copies(block, slot, source):
                    copy.start()

    def over_blocks(first_block, turns, step, ahead=None, before=None, behind=None):
        def visit(turn, carry):
            block = first_block + turn

            @pl.when(turn + 1 < turns)
            def _():
                fetch(block + 1, (turn + 1) % 2)

            whole = pair_ref.at[turn % 2]
            pltpu.make_async_copy(whole, whole, arrived.at[turn % 2]).wait()

            def units_of(index):
                first = index * 2 * UNROLL
                codes = [table_ref[block, 0, first + member] for member in range(2 * UNROLL)]
                return [codes[2 * unit : 2 * unit + 2] for unit in range(UNROLL)]

            def several(index, inner):
                step(turn % 2, units_of(index), units_of(index + 1) if ahead else None)
                return inner

            for index, chunk in enumerate(chunks):
                if before:
                    before(index)
                begins = table_ref[block, 1, chunk]
                if ahead:
                    ahead(turn % 2, units_of(begins))
                lax.fori_loop(begins, table_ref[block, 1, chunk + 1], several, 0)
                if behind:
                    behind(index)
            return carry

        if turns == 1:
            visit(0, 0)
        else:
            lax.fori_loop(0, turns, visit, 0)

    def frames_at(slot, unit):
        keys = []
        for code in unit:
            key_frame = code & ((1 << SHIFT) - 1)
            keys.append((slot, key_frame // frames_here, key_frame % frames_here))
        here = (unit[0] >> SHIFT) - first_frame
        return jnp.where((here >= 0) & (here < query_frames), here, 0), keys

    def scores_of(slot, unit):
        query_frame, keys = frames_at(slot, unit)
        held = jnp.concatenate([pair_ref[slot, device, 0, frame] for slot, device, frame in keys], axis=0)
        return lax.dot_general(
            wide_ref[query_frame], held, (((1,), (1,)), ((), ())), preferred_element_type=jnp.float32
        )

    def bias_of(unit):
        lane = lax.broadcasted_iota(jnp.int32, (1, PACKED), 1)
        bias = [jnp.where(code < DEAD, 0.0, NEVER) for code in unit]
        return jnp.where(lane < TOKF, bias[0], bias[1])

    def sums_of(keys, weights):
        held = jnp.concatenate([pair_ref[slot, device, 1, frame] for slot, device, frame in keys], axis=0)
        return by_head(
            jnp.dot(weights.astype(jnp.bfloat16), held, preferred_element_type=jnp.float32)
        )

    def by_head(both):
        lane = lax.broadcasted_iota(jnp.int32, (TOKF, LANES), 1)
        return jnp.where(lane < HDIM, both[:TOKF], both[TOKF:])

    def totals_of(weights):
        folded = weights[:, :LANES] + weights[:, LANES : 2 * LANES] + weights[:, 2 * LANES :]
        return by_head(folded + pltpu.roll(folded, HDIM, 1))

    def look_ahead(slot, units):
        for place, unit in enumerate(units):
            score_ref[place] = scores_of(slot, unit)

    def plain(slot, units, following):
        results = []
        for place, unit in enumerate(units):
            query_frame, keys = frames_at(slot, unit)
            weights = jnp.exp(score_ref[place] + bias_of(unit))
            score_ref[place] = scores_of(slot, following[place])
            results.append((query_frame, sums_of(keys, weights), totals_of(weights)))
        for query_frame, summed, total in results:
            sum_ref[query_frame] += summed
            total_ref[query_frame] += total

    asked = [
        pltpu.make_async_copy(ref, query_ref.at[index], left.at[index])
        for index, ref in enumerate(query_refs)
    ]
    for copy in asked:
        copy.start()
    fetch(begin, 0)
    frames_of = [pl.ds(index * frames_here, frames_here) for index in range(len(chunks))]
    taken, put = [], []
    for piece in range(states):
        old_refs = state_refs[2 * piece : 2 * piece + 2]
        pieces_chunks = old_refs[0].shape[0] // frames_here
        for index in range(pieces_chunks):
            if len(taken) == len(chunks):
                break
            begin_chunk = chunks[0] if states == 1 and pieces_chunks > len(chunks) else 0
            source = pl.ds((begin_chunk + index) * frames_here, frames_here)
            place = len(taken)
            taken.append(
                [
                    pltpu.make_async_copy(
                        old_ref.at[source], new_ref.at[frames_of[place]], arrived.at[2 + place]
                    )
                    for old_ref, new_ref in zip(old_refs, (sum_ref, total_ref))
                ]
            )
    for copies_here in taken:
        for copy in copies_here:
            copy.start()

    def widen(index):
        asked[index].wait()

        def one(frame, carry):
            rows = query_ref[index, frame] * jnp.asarray(HDIM**-0.5, wide_ref.dtype)
            first = lax.broadcasted_iota(jnp.int32, rows.shape, 1) < HDIM
            zeros = jnp.zeros_like(rows)
            wide_ref[index * frames_here + frame, :TOKF] = jnp.where(first, rows, zeros)
            wide_ref[index * frames_here + frame, TOKF:] = jnp.where(first, zeros, rows)
            return carry

        lax.fori_loop(0, frames_here, one, 0, unroll=4)

    def clear(frame, carry):
        sum_ref[frame] = jnp.zeros(sum_ref.shape[1:], sum_ref.dtype)
        total_ref[frame] = jnp.zeros(total_ref.shape[1:], total_ref.dtype)
        return carry

    for index in range(len(chunks)):
        widen(index)
    if not states:
        lax.fori_loop(0, query_frames, clear, 0, unroll=4)

    def enter(index):
        if states:
            for ref in (sum_ref, total_ref):
                part = ref.at[frames_of[index]]
                pltpu.make_async_copy(part, part, arrived.at[2 + index]).wait()

    def leave(index):
        if not ends:
            for ref, out in zip((sum_ref, total_ref), out_refs):
                copy = pltpu.make_async_copy(
                    ref.at[frames_of[index]], out.at[frames_of[index]], left.at[index]
                )
                copy.start()
                put.append(copy)

    if number == 1:
        over_blocks(begin, number, plain, look_ahead, enter, leave)
    else:
        for index in range(len(chunks)):
            enter(index)
        over_blocks(begin, number, plain, look_ahead)
        for index in range(len(chunks)):
            leave(index)
    for copy in put:
        copy.wait()
    if not ends:
        return
    whole_ref, top_ref = refs[8:]

    def gather_totals(frame, carry):
        total = total_ref[frame]
        square = (LANES, LANES)
        same = lax.broadcasted_iota(jnp.int32, square, 0) // HDIM == lax.broadcasted_iota(jnp.int32, square, 1) // HDIM
        ones = jnp.where(same, 1.0, 0.0).astype(jnp.bfloat16)
        high = total.astype(jnp.bfloat16)
        low = (total - high.astype(jnp.float32)).astype(jnp.bfloat16)
        whole_ref[frame] = jnp.dot(high, ones, preferred_element_type=jnp.float32) + jnp.dot(
            low, ones, preferred_element_type=jnp.float32
        )
        return carry

    lax.fori_loop(0, query_frames, gather_totals, 0, unroll=4)
    within = (jnp.min(whole_ref[...]) > LOW) & (jnp.max(whole_ref[...]) < HIGH)

    @pl.when(jnp.logical_not(within))
    def _():
        lax.fori_loop(0, query_frames, clear, 0)
        top_ref[...] = jnp.full_like(top_ref, 2 * NEVER)

        def shifted(slot, units, _):
            for unit in units:
                query_frame, keys = frames_at(slot, unit)
                scores = scores_of(slot, unit) + bias_of(unit)
                old = top_ref[query_frame]
                new = jnp.maximum(old, jnp.max(scores, axis=1, keepdims=True))
                keep = by_head(jnp.exp(old - new))
                weights = jnp.exp(scores - new[:, :1])
                sum_ref[query_frame] = sum_ref[query_frame] * keep + sums_of(keys, weights)
                total_ref[query_frame] = total_ref[query_frame] * keep + totals_of(weights)
                top_ref[query_frame] = new

        fetch(0, 0)
        over_blocks(0, len(sources) * per_source, shifted)
        lax.fori_loop(0, query_frames, gather_totals, 0)

    for index, out_ref in enumerate(out_refs):

        def finish(frame, carry):
            here = index * frames_here + frame
            out_ref[frame] = (sum_ref[here] / whole_ref[here]).astype(out_ref.dtype)
            return carry

        lax.fori_loop(0, frames_here, finish, 0, unroll=4)


def attend(queries, chunks, pairs, table, places, order, begin, number, group, state, ends):
    frames_here = queries[0].shape[0]
    shape = (len(chunks) * frames_here, TOKF, LANES)
    held = jax.ShapeDtypeStruct(shape, jnp.float32)
    whole = pl.BlockSpec(memory_space=pltpu.VMEM)
    scalars = pl.BlockSpec(memory_space=pltpu.SMEM)
    stays = pl.BlockSpec(memory_space=pltpu.HBM)
    room = pltpu.VMEM(shape, jnp.float32)
    wide = (shape[0], PACKED, LANES)
    common = [
        pltpu.VMEM((2, group) + pairs[0][0].shape[1:], queries[0].dtype),
        pltpu.VMEM(wide, queries[0].dtype),
        pltpu.VMEM((len(chunks),) + queries[0].shape, queries[0].dtype),
        pltpu.VMEM((UNROLL, PACKED, PACKED), jnp.float32),
        pltpu.SemaphoreType.DMA((2 + len(chunks),)),
        pltpu.SemaphoreType.DMA((len(chunks),)),
    ]
    listed = [array for plane in pairs for array in plane] + [array for pair in state for array in pair]
    return pl.pallas_call(
        functools.partial(
            attend_kernel,
            begin,
            number,
            tuple(chunks),
            tuple(len(plane) for plane in pairs),
            len(state),
            ends,
        ),
        in_specs=[scalars, scalars] + [stays] * (1 + len(queries) + len(listed)),
        out_specs=[whole] + ([whole] * len(chunks) if ends else [stays, stays]),
        out_shape=[jax.ShapeDtypeStruct(order.shape, order.dtype)]
        + (
            [jax.ShapeDtypeStruct(query.shape, query.dtype) for query in queries]
            if ends
            else [held, held]
        ),
        scratch_shapes=[room] * 2
        + common
        + ([room, pltpu.VMEM(wide, jnp.float32)] if ends else []),
        compiler_params=pltpu.CompilerParams(vmem_limit_bytes=VMEM_LIMIT),
        cost_estimate=pl.CostEstimate(flops=1, bytes_accessed=1, transcendentals=0),
    )(table, places, order, *queries, *listed)


def project_kernel(parts, place_ref, near_ref, far_ref, *refs):
    plane, side = place_ref[0], place_ref[2]
    out_ref = refs[2 * parts]
    columns = out_ref.shape[1]
    mine = pl.ds(pl.multiple_of(side * columns, columns), columns)
    rows = [pl.ds(pl.multiple_of((plane ^ part) * LANES, LANES), LANES) for part in range(parts)]
    merged = jnp.concatenate([ref[...] for ref in refs[: 2 * parts]], axis=1)
    weight = [near_ref[row, mine] for row in rows] + [far_ref[row, :] for row in rows]
    out_ref[...] = jnp.dot(
        merged, jnp.concatenate(weight, axis=0), preferred_element_type=jnp.float32
    ).astype(out_ref.dtype)


def project(merged, others, near, far, places):
    rows = merged[0].shape[0]
    tile = rows // 4 if rows % 64 == 0 else rows
    parts = merged + others
    columns = far.shape[1]
    return pl.pallas_call(
        functools.partial(project_kernel, len(merged)),
        grid=(rows // tile,),
        in_specs=[pl.BlockSpec(memory_space=pltpu.SMEM)]
        + [pl.BlockSpec(weight.shape, lambda row: (0, 0)) for weight in (near, far)]
        + [pl.BlockSpec((tile, part.shape[1]), lambda row: (row, 0)) for part in parts],
        out_specs=pl.BlockSpec((tile, columns), lambda row: (row, 0)),
        out_shape=jax.ShapeDtypeStruct((rows, columns), parts[0].dtype),
        compiler_params=pltpu.CompilerParams(vmem_limit_bytes=VMEM_LIMIT),
        cost_estimate=pl.CostEstimate(
            flops=4 * rows * far.size, bytes_accessed=rows * 4096, transcendentals=0
        ),
    )(places, near, far, *parts)


def spread(queries, pairs, far, table, places, swap, across, gather, plane_size):
    chunk_order = [0, 3, 1, 2]
    barrier = lax.optimization_barrier
    order = jnp.zeros((8, LANES), jnp.int32)

    def run(distances, plane, keyed, state, ends=False, number=1):
        return attend(
            [queries[distance] for distance in distances],
            [chunk_order.index(distance) for distance in distances],
            keyed if ends else keyed[plane : plane + number],
            table,
            places,
            order,
            plane,
            number,
            plane_size,
            state,
            ends,
        )

    def gathered(distance):
        return [gather(pairs[distance], plane_size)]

    keyed = [gathered(0), None, None, None]
    pairs[1], asked = swap(pairs[1], 1), swap(jnp.stack([queries[3], pairs[3][0]]), 3)
    pairs[1], asked, valued, queries[1], table = barrier(
        (pairs[1], asked, pairs[3][1], queries[1], table)
    )
    keyed[1] = gathered(1)
    valued, queries[1] = swap(valued, 3), swap(queries[1], 1)
    valued, asked, queries[1], pairs[2], far, order = barrier(
        (valued, asked, queries[1], pairs[2], far, order)
    )
    queries[3], pairs[3] = asked[0], jnp.stack([asked[1], valued])
    keyed[3] = gathered(3)
    pairs[2], far = swap(pairs[2], 2), across(far)
    order, *state = run([0, 3, 1], 0, keyed, [])
    order, *state = run([0, 3, 1], 1, keyed, [state])
    pairs[2], queries[2], far, order = barrier((pairs[2], queries[2], far, order))
    keyed[2] = gathered(2)
    queries[2] = swap(queries[2], 2)
    order, *state = run([0, 3, 1], 3, keyed, [state])
    queries[2], order = barrier((queries[2], order))
    order, *last = run([2], 0, keyed, [], number=2)
    merged, others = [None] * 4, [None] * 4

    def rows_of(out):
        return out.reshape(-1, LANES)

    order, out, near_out = run([3, 1], 2, keyed, [state], True)
    out, near_out, order = barrier((rows_of(out), rows_of(near_out), order))
    merged[3], merged[1] = swap(out, 3), swap(near_out, 1)
    order, out = run([2], 2, keyed, [last], True, 2)
    out, merged[3], merged[1], order = barrier((rows_of(out), merged[3], merged[1], order))
    merged[2], others[3], others[1] = swap(out, 2), across(merged[3]), across(merged[1])
    order, out = run([0], 2, keyed, [state], True)
    merged[0], others[3] = barrier((rows_of(out), others[3]))
    others[0], others[2] = across(merged[0]), across(merged[2])
    return merged, others, far


def body(query_states, key_states, value_states, pair_list, out_weight):
    peers = lax.axis_size("frames")
    my_index = lax.axis_index("frames")
    rows, columns = query_states.shape
    frames_here = rows // TOKF
    planes = columns // LANES
    plane_size = peers // planes
    group = min(plane_size, GROUP)
    plane, place = my_index // plane_size, my_index % plane_size
    side = lax.axis_index("heads")
    places = jnp.stack([plane, place, side]).astype(jnp.int32)
    table = attend_table(pair_list, planes, plane_size, group, frames_here, places)
    per_plane = plane_size // group

    def swap(array, distance, axis=plane_size):
        if distance == 0:
            return array
        return lax.ppermute(
            array, "frames", [(index, index ^ (distance * axis)) for index in range(peers)]
        )

    def gather(array, size):
        members = [list(range(start, start + size)) for start in range(0, peers, size)]
        return lax.all_gather(array, "frames", axis_index_groups=members)

    def across(array):
        return lax.ppermute(array, "heads", [(0, 1), (1, 0)])

    def columns_of(array, distance):
        chosen = lax.dynamic_slice_in_dim(array, (plane ^ distance) * LANES, LANES, 1)
        return chosen.reshape(frames_here, TOKF, LANES)

    queries = [columns_of(query_states, distance) for distance in range(planes)]
    pairs = [
        jnp.stack([columns_of(key_states, distance), columns_of(value_states, distance)])
        for distance in range(planes)
    ]
    two = lax.axis_size("heads") == 2
    far = lax.dynamic_slice_in_dim(out_weight, (1 - side) * columns, columns, 1)
    if planes == 1:
        keyed = [[gather(pairs[0], plane_size)]]
        order = jnp.zeros((8, LANES), jnp.int32)
        _, out = attend(
            queries, [0], keyed, table, places, order, 0, per_plane, group, [], True
        )
        out = out.reshape(rows, LANES)
        if not two:
            term = jnp.dot(out, out_weight, preferred_element_type=jnp.float32)
            return lax.psum_scatter(
                term.astype(out.dtype), "heads", scatter_dimension=1, tiled=True
            )
        return project([out], [across(out)], out_weight, across(far), places)
    assert two
    merged, others, far = spread(
        queries, pairs, far, table, places, swap, across, gather, plane_size
    )
    return project(merged, others, out_weight, far, places)


def solution(mesh):
    placed = (
        P("frames", "heads"),
        P("frames", "heads"),
        P("frames", "heads"),
        P(),
        P("heads", None),
    )
    return jax.shard_map(
        body, mesh=mesh, in_specs=placed, out_specs=P("frames", "heads"), check_vma=False
    )
```

```python
import functools

import jax
import jax.numpy as jnp
from jax import lax
from jax.experimental import pallas as pl
from jax.experimental.pallas import tpu as pltpu
from jax.sharding import PartitionSpec as P

HDIM = 64
TOKF = 192
LANES = 128
PACKED = 2 * TOKF
GROUP = 4
SHIFT = 16
DEAD = 1 << 30
UNROLL = 2
LOW, HIGH = 2.0**-60, 2.0**100
NEVER = -1e30
VMEM_LIMIT = 60 * 1024 * 1024


def table_kernel(planes, plane_size, group, frames_here, place_ref, ends_ref, table_ref):
    block = pl.program_id(0)
    plane, place = place_ref[0], place_ref[1]
    assert planes in (1, 4)
    plane_frames = plane_size * frames_here
    key_frames = group * frames_here
    query_frames = planes * frames_here
    width = table_ref.shape[2]
    tiles = ends_ref.shape[1]
    step = 2 * UNROLL

    def bits(size):
        assert size & (size - 1) == 0
        return size.bit_length() - 1

    def iota(shape, axis):
        return lax.broadcasted_iota(jnp.int32, shape, axis)

    candidates = []
    for side in range(2):
        for tile in range(tiles):
            pair = [ends_ref[end, tile : tile + 1] ^ (plane << bits(plane_frames)) for end in (side, 1 - side)]
            candidates.append((pair[0], pair[1], None))
    lane = iota((1, LANES), 1)
    chunk = lane >> bits(frames_here)
    mine = (
        ((((chunk & 1) << 1) + (((chunk >> 1) ^ chunk) & 1)) << bits(plane_frames))
        + (place << bits(frames_here))
        + (lane & (frames_here - 1))
    )
    candidates.append((mine, mine, lane < query_frames))

    lives, queries, keys, hits = [], [], [], []
    for asked, key, valid in candidates:
        live = (key >> bits(key_frames) == block) & (
            (asked >> bits(frames_here)) & (plane_size - 1) == place
        )
        if valid is not None:
            live = live & valid
        distance = asked >> bits(plane_frames)
        chunk = ((distance ^ (distance >> 1)) & 1) * 2 + (distance >> 1)
        query = (chunk << bits(frames_here)) + (asked & (frames_here - 1))
        query = jnp.where(live, query, query_frames)
        lives.append(live)
        queries.append(query)
        keys.append(key & (key_frames - 1))
        hits.append(jnp.where(query == iota((query_frames, LANES), 0), 1.0, 0.0))
    stacked = jnp.concatenate(hits, axis=0).astype(jnp.bfloat16)

    def product(left, right):
        return jnp.dot(left.astype(jnp.bfloat16), right.astype(jnp.bfloat16), preferred_element_type=jnp.float32)

    def ones_where(condition):
        return jnp.where(condition, 1.0, 0.0)

    square = (LANES, LANES)
    earlier = product(stacked, ones_where(iota(square, 0) < iota(square, 1)))
    every = product(stacked, jnp.ones(square, jnp.float32))
    before = [jnp.zeros((query_frames, LANES), jnp.float32)]
    for tile in range(len(hits)):
        before.append(before[-1] + every[tile * query_frames : (tile + 1) * query_frames])
    used = 2.0 * jnp.floor((before[-1] + 1.0) * 0.5)
    square = (query_frames, query_frames)
    row, column = iota(square, 0), iota(square, 1)
    row_chunk, column_chunk = row >> bits(frames_here), column >> bits(frames_here)
    inside = product(ones_where((row_chunk == column_chunk) & (column < row)), used)
    whole = product(ones_where(row_chunk == column_chunk), used)
    steps = jnp.floor((whole + (step - 1.0)) * (1.0 / step))
    leads = column & (frames_here - 1) == 0
    chunk_start = product(ones_where((column_chunk < row_chunk) & leads), steps)
    start = inside + step * chunk_start

    frame = iota((query_frames, LANES), 0)
    at = iota((query_frames, LANES), 1)
    first = frame & (frames_here - 1) == 0
    starts = jnp.where(first & (at == frame >> bits(frames_here)), chunk_start, 0.0)
    starts = starts + jnp.where(first & (at == planes), steps, 0.0)
    starts = jnp.sum(starts, axis=0, keepdims=True).astype(jnp.int32)

    placed, values = [], []
    for tile, hit in enumerate(hits):
        rank = earlier[tile * query_frames : (tile + 1) * query_frames] + before[tile] + start
        slot = jnp.sum(hit * rank, axis=0, keepdims=True).astype(jnp.int32)
        slot = jnp.where(lives[tile], slot, -1)
        placed.append(ones_where(slot == iota((width, LANES), 0)).astype(jnp.bfloat16))
        kind = iota((8, LANES), 0)
        value = jnp.where(kind == 0, queries[tile], jnp.where(kind == 1, keys[tile], 1))
        values.append(value.astype(jnp.float32).astype(jnp.bfloat16))
    codes = lax.dot_general(
        jnp.concatenate(values, axis=1),
        jnp.concatenate(placed, axis=1),
        (((1,), (1,)), ((), ())),
        preferred_element_type=jnp.float32,
    ).astype(jnp.int32)
    code = jnp.where(codes[2:3] > 0, (codes[0:1] << SHIFT) + codes[1:2], DEAD)
    starts = jnp.concatenate([starts] * (width // LANES), axis=1)
    table_ref[0] = jnp.where(iota((2, width), 0) == 0, code, starts)


def attend_table(pair_list, planes, plane_size, group, frames_here, places):
    peers = planes * plane_size
    rows = pair_list.shape[0]
    blocks = peers // group
    number = 2 * planes * group * (rows // peers // peers) + frames_here
    most = number + planes * frames_here + planes * (2 * UNROLL - 2)
    width = (most + LANES - 1) // LANES * LANES
    ends = pair_list.T.reshape(2, rows // LANES, LANES)
    return pl.pallas_call(
        functools.partial(table_kernel, planes, plane_size, group, frames_here),
        grid=(blocks,),
        in_specs=[
            pl.BlockSpec(memory_space=pltpu.SMEM),
            pl.BlockSpec(ends.shape, lambda block: (0, 0, 0)),
        ],
        out_specs=pl.BlockSpec((1, 2, width), lambda block: (block, 0, 0)),
        out_shape=jax.ShapeDtypeStruct((blocks, 2, width), jnp.int32),
        compiler_params=pltpu.CompilerParams(vmem_limit_bytes=VMEM_LIMIT),
    )(places, ends)


def attend_kernel(
    begin, number, chunks, sources, states, ends, table_ref, place_ref, order_ref, *refs
):
    del order_ref
    query_refs, refs = refs[: len(chunks)], refs[len(chunks) :]
    pair_refs = []
    for parts in sources:
        pair_refs.append(refs[:parts])
        refs = refs[parts:]
    state_refs, refs = refs[: 2 * states], refs[2 * states :]
    done_ref, refs = refs[0], refs[1:]
    done_ref[...] = jnp.zeros_like(done_ref)
    outs = len(chunks) if ends else 2
    out_refs, refs = refs[:outs], refs[outs:]
    sum_ref, total_ref, pair_ref, wide_ref, query_ref, score_ref, arrived, left = refs[:8]
    frames_here = query_refs[0].shape[0]
    group = pair_ref.shape[2]
    per_source = max(pair_refs[0][0].shape[0] // group, 1)
    first_frame = chunks[0] * frames_here
    query_frames = len(chunks) * frames_here
    held_from = 0 if ends else begin

    def copies(block, slot, source):
        refs_here = pair_refs[source]
        devices = pl.ds(block % per_source * group, group)
        return [
            pltpu.make_async_copy(
                refs_here[0].at[devices, kind], pair_ref.at[slot, kind], arrived.at[2 * slot + kind]
            )
            for kind in range(2)
        ]

    def fetch(block, slot):
        for source in range(len(sources)):

            @pl.when((block - held_from) // per_source == source)
            def _():
                for copy in copies(block, slot, source):
                    copy.start()

    def over_blocks(first_block, turns, step, ahead=None, before=None, behind=None):
        def visit(turn, carry):
            block = first_block + turn

            @pl.when(turn + 1 < turns)
            def _():
                fetch(block + 1, (turn + 1) % 2)

            def wait_for(kind):
                here = pair_ref.at[turn % 2, kind]
                pltpu.make_async_copy(here, here, arrived.at[2 * (turn % 2) + kind]).wait()

            wait_for(0)

            def units_of(index):
                first = index * 2 * UNROLL
                codes = [table_ref[block, 0, first + member] for member in range(2 * UNROLL)]
                return [codes[2 * unit : 2 * unit + 2] for unit in range(UNROLL)]

            def several(index, inner):
                step(turn % 2, units_of(index), units_of(index + 1) if ahead else None)
                return inner

            for index, chunk in enumerate(chunks):
                if before:
                    before(index)
                begins = table_ref[block, 1, chunk]
                if ahead:
                    ahead(turn % 2, units_of(begins))
                if index == 0:
                    wait_for(1)
                lax.fori_loop(begins, table_ref[block, 1, chunk + 1], several, 0)
                if behind:
                    behind(index)
            return carry

        if turns == 1:
            visit(0, 0)
        else:
            lax.fori_loop(0, turns, visit, 0)

    def frames_at(slot, unit):
        keys = []
        for code in unit:
            key_frame = code & ((1 << SHIFT) - 1)
            keys.append((slot, key_frame // frames_here, key_frame % frames_here))
        here = (unit[0] >> SHIFT) - first_frame
        return jnp.where((here >= 0) & (here < query_frames), here, 0), keys

    def scores_of(slot, unit):
        query_frame, keys = frames_at(slot, unit)
        held = jnp.concatenate([pair_ref[slot, 0, device, frame] for slot, device, frame in keys], axis=0)
        return lax.dot_general(
            wide_ref[query_frame], held, (((1,), (1,)), ((), ())), preferred_element_type=jnp.float32
        )

    def bias_of(unit):
        lane = lax.broadcasted_iota(jnp.int32, (1, PACKED), 1)
        bias = [jnp.where(code < DEAD, 0.0, NEVER) for code in unit]
        return jnp.where(lane < TOKF, bias[0], bias[1])

    def sums_of(keys, weights):
        held = jnp.concatenate([pair_ref[slot, 1, device, frame] for slot, device, frame in keys], axis=0)
        return by_head(
            jnp.dot(weights.astype(jnp.bfloat16), held, preferred_element_type=jnp.float32)
        )

    def by_head(both):
        lane = lax.broadcasted_iota(jnp.int32, (TOKF, LANES), 1)
        return jnp.where(lane < HDIM, both[:TOKF], both[TOKF:])

    def totals_of(weights):
        folded = weights[:, :LANES] + weights[:, LANES : 2 * LANES] + weights[:, 2 * LANES :]
        return by_head(folded + pltpu.roll(folded, HDIM, 1))

    def look_ahead(slot, units):
        for place, unit in enumerate(units):
            score_ref[place] = scores_of(slot, unit)

    def plain(slot, units, following):
        results = []
        for place, unit in enumerate(units):
            query_frame, keys = frames_at(slot, unit)
            weights = jnp.exp(score_ref[place] + bias_of(unit))
            score_ref[place] = scores_of(slot, following[place])
            results.append((query_frame, sums_of(keys, weights), totals_of(weights)))
        for query_frame, summed, total in results:
            sum_ref[query_frame] += summed
            total_ref[query_frame] += total

    asked = [
        pltpu.make_async_copy(ref, query_ref.at[index], left.at[index])
        for index, ref in enumerate(query_refs)
    ]
    for copy in asked:
        copy.start()
    fetch(begin, 0)
    frames_of = [pl.ds(index * frames_here, frames_here) for index in range(len(chunks))]
    taken, put = [], []
    for piece in range(states):
        old_refs = state_refs[2 * piece : 2 * piece + 2]
        pieces_chunks = old_refs[0].shape[0] // frames_here
        for index in range(pieces_chunks):
            if len(taken) == len(chunks):
                break
            begin_chunk = chunks[0] if states == 1 and pieces_chunks > len(chunks) else 0
            source = pl.ds((begin_chunk + index) * frames_here, frames_here)
            place = len(taken)
            taken.append(
                [
                    pltpu.make_async_copy(
                        old_ref.at[source], new_ref.at[frames_of[place]], arrived.at[4 + place]
                    )
                    for old_ref, new_ref in zip(old_refs, (sum_ref, total_ref))
                ]
            )
    for copies_here in taken:
        for copy in copies_here:
            copy.start()

    def widen(index):
        asked[index].wait()

        def one(frame, carry):
            rows = query_ref[index, frame] * jnp.asarray(HDIM**-0.5, wide_ref.dtype)
            first = lax.broadcasted_iota(jnp.int32, rows.shape, 1) < HDIM
            zeros = jnp.zeros_like(rows)
            wide_ref[index * frames_here + frame, :TOKF] = jnp.where(first, rows, zeros)
            wide_ref[index * frames_here + frame, TOKF:] = jnp.where(first, zeros, rows)
            return carry

        lax.fori_loop(0, frames_here, one, 0, unroll=4)

    def clear(frame, carry):
        sum_ref[frame] = jnp.zeros(sum_ref.shape[1:], sum_ref.dtype)
        total_ref[frame] = jnp.zeros(total_ref.shape[1:], total_ref.dtype)
        return carry

    for index in range(len(chunks)):
        widen(index)
    if not states:
        lax.fori_loop(0, query_frames, clear, 0, unroll=4)

    def enter(index):
        if states:
            for ref in (sum_ref, total_ref):
                part = ref.at[frames_of[index]]
                pltpu.make_async_copy(part, part, arrived.at[4 + index]).wait()

    def leave(index):
        if not ends:
            for ref, out in zip((sum_ref, total_ref), out_refs):
                copy = pltpu.make_async_copy(
                    ref.at[frames_of[index]], out.at[frames_of[index]], left.at[index]
                )
                copy.start()
                put.append(copy)

    if number == 1:
        over_blocks(begin, number, plain, look_ahead, enter, leave)
    else:
        for index in range(len(chunks)):
            enter(index)
        over_blocks(begin, number, plain, look_ahead)
        for index in range(len(chunks)):
            leave(index)
    for copy in put:
        copy.wait()
    if not ends:
        return
    whole_ref, top_ref = refs[8:]

    def gather_totals(frame, carry):
        total = total_ref[frame]
        square = (LANES, LANES)
        same = lax.broadcasted_iota(jnp.int32, square, 0) // HDIM == lax.broadcasted_iota(jnp.int32, square, 1) // HDIM
        ones = jnp.where(same, 1.0, 0.0).astype(jnp.bfloat16)
        high = total.astype(jnp.bfloat16)
        low = (total - high.astype(jnp.float32)).astype(jnp.bfloat16)
        whole_ref[frame] = jnp.dot(high, ones, preferred_element_type=jnp.float32) + jnp.dot(
            low, ones, preferred_element_type=jnp.float32
        )
        return carry

    lax.fori_loop(0, query_frames, gather_totals, 0, unroll=4)
    within = (jnp.min(whole_ref[...]) > LOW) & (jnp.max(whole_ref[...]) < HIGH)

    @pl.when(jnp.logical_not(within))
    def _():
        lax.fori_loop(0, query_frames, clear, 0)
        top_ref[...] = jnp.full_like(top_ref, 2 * NEVER)

        def shifted(slot, units, _):
            for unit in units:
                query_frame, keys = frames_at(slot, unit)
                scores = scores_of(slot, unit) + bias_of(unit)
                old = top_ref[query_frame]
                new = jnp.maximum(old, jnp.max(scores, axis=1, keepdims=True))
                keep = by_head(jnp.exp(old - new))
                weights = jnp.exp(scores - new[:, :1])
                sum_ref[query_frame] = sum_ref[query_frame] * keep + sums_of(keys, weights)
                total_ref[query_frame] = total_ref[query_frame] * keep + totals_of(weights)
                top_ref[query_frame] = new

        fetch(0, 0)
        over_blocks(0, len(sources) * per_source, shifted)
        lax.fori_loop(0, query_frames, gather_totals, 0)

    for index, out_ref in enumerate(out_refs):

        def finish(frame, carry):
            here = index * frames_here + frame
            out_ref[frame] = (sum_ref[here] / whole_ref[here]).astype(out_ref.dtype)
            return carry

        lax.fori_loop(0, frames_here, finish, 0, unroll=4)


def attend(queries, chunks, pairs, table, places, order, begin, number, group, state, ends):
    frames_here = queries[0].shape[0]
    shape = (len(chunks) * frames_here, TOKF, LANES)
    held = jax.ShapeDtypeStruct(shape, jnp.float32)
    whole = pl.BlockSpec(memory_space=pltpu.VMEM)
    scalars = pl.BlockSpec(memory_space=pltpu.SMEM)
    stays = pl.BlockSpec(memory_space=pltpu.HBM)
    room = pltpu.VMEM(shape, jnp.float32)
    wide = (shape[0], PACKED, LANES)
    common = [
        pltpu.VMEM((2, 2, group) + pairs[0][0].shape[2:], queries[0].dtype),
        pltpu.VMEM(wide, queries[0].dtype),
        pltpu.VMEM((len(chunks),) + queries[0].shape, queries[0].dtype),
        pltpu.VMEM((UNROLL, PACKED, PACKED), jnp.float32),
        pltpu.SemaphoreType.DMA((4 + len(chunks),)),
        pltpu.SemaphoreType.DMA((len(chunks),)),
    ]
    listed = [array for plane in pairs for array in plane] + [array for pair in state for array in pair]
    return pl.pallas_call(
        functools.partial(
            attend_kernel,
            begin,
            number,
            tuple(chunks),
            tuple(len(plane) for plane in pairs),
            len(state),
            ends,
        ),
        in_specs=[scalars, scalars] + [stays] * (1 + len(queries) + len(listed)),
        out_specs=[whole] + ([whole] * len(chunks) if ends else [stays, stays]),
        out_shape=[jax.ShapeDtypeStruct(order.shape, order.dtype)]
        + (
            [jax.ShapeDtypeStruct(query.shape, query.dtype) for query in queries]
            if ends
            else [held, held]
        ),
        scratch_shapes=[room] * 2
        + common
        + ([room, pltpu.VMEM(wide, jnp.float32)] if ends else []),
        compiler_params=pltpu.CompilerParams(vmem_limit_bytes=VMEM_LIMIT),
        cost_estimate=pl.CostEstimate(flops=1, bytes_accessed=1, transcendentals=0),
    )(table, places, order, *queries, *listed)


def project_kernel(parts, place_ref, *refs):
    del place_ref
    row_refs, weight_refs, refs = refs[:parts], refs[parts : 2 * parts], refs[2 * parts :]
    out_ref = refs[-1]
    total = jnp.dot(
        jnp.concatenate([ref[...] for ref in row_refs], axis=1),
        jnp.concatenate([ref[...] for ref in weight_refs], axis=0),
        preferred_element_type=jnp.float32,
    )
    if len(refs) > 1:
        total = total + refs[0][...]
    out_ref[...] = total.astype(out_ref.dtype)


def project(parts, near, far, places, total, ends):
    rows = parts[0][2].shape[0]
    tile = rows // 4 if rows % 64 == 0 else rows
    columns = far.shape[1]

    def weight_spec(other, distance):
        def place(row, at):
            return (at[0] ^ distance, 0 if other else at[2])

        return pl.BlockSpec((LANES, columns), place)

    kept = pl.BlockSpec((tile, columns), lambda row, at: (row, 0))
    return pl.pallas_call(
        functools.partial(project_kernel, len(parts)),
        grid_spec=pltpu.PrefetchScalarGridSpec(
            num_scalar_prefetch=1,
            grid=(rows // tile,),
            in_specs=[pl.BlockSpec((tile, LANES), lambda row, at: (row, 0)) for _ in parts]
            + [weight_spec(other, distance) for other, distance, _ in parts]
            + ([] if total is None else [kept]),
            out_specs=kept,
        ),
        out_shape=jax.ShapeDtypeStruct((rows, columns), near.dtype if ends else jnp.float32),
        compiler_params=pltpu.CompilerParams(vmem_limit_bytes=VMEM_LIMIT),
        cost_estimate=pl.CostEstimate(flops=1, bytes_accessed=1, transcendentals=0),
    )(
        places,
        *(part for _, _, part in parts),
        *(far if other else near for other, _, _ in parts),
        *(() if total is None else (total,)),
    )


def spread(queries, pairs, far, table, places, swap, across, gather, plane_size):
    chunk_order = [0, 3, 1, 2]
    barrier = lax.optimization_barrier
    order = jnp.zeros((8, LANES), jnp.int32)

    def run(distances, plane, keyed, state, ends=False, number=1):
        return attend(
            [queries[distance] for distance in distances],
            [chunk_order.index(distance) for distance in distances],
            keyed if ends else keyed[plane : plane + number],
            table,
            places,
            order,
            plane,
            number,
            plane_size,
            state,
            ends,
        )

    def gathered(distance):
        return [gather(pairs[distance], plane_size)]

    keyed = [gathered(0), None, None, None]
    pairs[1], queries[3] = swap(pairs[1], 1), swap(queries[3], 3)
    pairs[1], queries[3], queries[1], pairs[3], table, far, order = barrier(
        (pairs[1], queries[3], queries[1], pairs[3], table, far, order)
    )
    keyed[1] = gathered(1)
    pairs[3], queries[1], far = swap(pairs[3], 3), swap(queries[1], 1), across(far)
    order, *early = run([0, 3], 0, keyed, [])
    queries[1], far, order = barrier((queries[1], far, order))
    order, *late = run([1], 0, keyed, [])
    pairs[3], pairs[2], order = barrier((pairs[3], pairs[2], order))
    keyed[3] = gathered(3)
    pairs[2] = swap(pairs[2], 2)
    order, *state = run([0, 3, 1], 1, keyed, [early, late])
    pairs[2], queries[2], order = barrier((pairs[2], queries[2], order))
    keyed[2] = gathered(2)
    queries[2] = swap(queries[2], 2)
    order, *state = run([0, 3, 1], 3, keyed, [state])
    queries[2], order = barrier((queries[2], order))
    order, *last = run([2], 0, keyed, [], number=2)
    merged, others = [None] * 4, [None] * 4

    def rows_of(out):
        return out.reshape(-1, LANES)

    order, *outs = run([0, 3, 1], 2, keyed, [state], True)
    merged[0], out, near_out, order = barrier(tuple(map(rows_of, outs)) + (order,))
    merged[3], merged[1], others[0] = swap(out, 3), swap(near_out, 1), across(merged[0])
    order, out = run([2], 2, keyed, [last], True, 2)
    out, merged[3], merged[1], others[0] = barrier(
        (rows_of(out), merged[3], merged[1], others[0])
    )
    merged[2], others[1], others[3] = swap(out, 2), across(merged[1]), across(merged[3])
    others[2] = across(merged[2])
    return merged, others, far


def body(query_states, key_states, value_states, pair_list, out_weight):
    peers = lax.axis_size("frames")
    my_index = lax.axis_index("frames")
    rows, columns = query_states.shape
    frames_here = rows // TOKF
    planes = columns // LANES
    plane_size = peers // planes
    group = min(plane_size, GROUP)
    plane, place = my_index // plane_size, my_index % plane_size
    side = lax.axis_index("heads")
    places = jnp.stack([plane, place, side]).astype(jnp.int32)
    table = attend_table(pair_list, planes, plane_size, group, frames_here, places)
    per_plane = plane_size // group

    def swap(array, distance, axis=plane_size):
        if distance == 0:
            return array
        return lax.ppermute(
            array, "frames", [(index, index ^ (distance * axis)) for index in range(peers)]
        )

    def gather(array, size):
        members = [list(range(start, start + size)) for start in range(0, peers, size)]
        return lax.all_gather(array, "frames", axis_index_groups=members)

    def across(array):
        return lax.ppermute(array, "heads", [(0, 1), (1, 0)])

    def columns_of(array, distance):
        chosen = lax.dynamic_slice_in_dim(array, (plane ^ distance) * LANES, LANES, 1)
        return chosen.reshape(frames_here, TOKF, LANES)

    queries = [columns_of(query_states, distance) for distance in range(planes)]
    pairs = [
        jnp.stack([columns_of(key_states, distance), columns_of(value_states, distance)])
        for distance in range(planes)
    ]
    two = lax.axis_size("heads") == 2
    far = lax.dynamic_slice_in_dim(out_weight, (1 - side) * columns, columns, 1)
    if planes == 1:
        keyed = [[gather(pairs[0], plane_size)]]
        order = jnp.zeros((8, LANES), jnp.int32)
        _, out = attend(
            queries, [0], keyed, table, places, order, 0, per_plane, group, [], True
        )
        out = out.reshape(rows, LANES)
        if not two:
            term = jnp.dot(out, out_weight, preferred_element_type=jnp.float32)
            return lax.psum_scatter(
                term.astype(out.dtype), "heads", scatter_dimension=1, tiled=True
            )
        parts = [(False, 0, out), (True, 0, across(out))]
        return project(parts, out_weight, across(far), places, None, True)
    assert two
    merged, others, far = spread(
        queries, pairs, far, table, places, swap, across, gather, plane_size
    )
    ready = [(False, distance, merged[distance]) for distance in range(planes)]
    ready += [(True, distance, others[distance]) for distance in (0, 1, 3)]
    total = project(ready, out_weight, far, places, None, False)
    return project([(True, 2, others[2])], out_weight, far, places, total, True)


def solution(mesh):
    placed = (
        P("frames", "heads"),
        P("frames", "heads"),
        P("frames", "heads"),
        P(),
        P("heads", None),
    )
    return jax.shard_map(
        body, mesh=mesh, in_specs=placed, out_specs=P("frames", "heads"), check_vma=False
    )
```

```python
import functools

import jax
import jax.numpy as jnp
from jax import lax
from jax.experimental import pallas as pl
from jax.experimental.pallas import tpu as pltpu
from jax.sharding import PartitionSpec as P

HDIM = 64
TOKF = 192
LANES = 128
PACKED = 2 * TOKF
GROUP = 4
SHIFT = 16
DEAD = 1 << 30
UNROLL = 2
LOW, HIGH = 2.0**-60, 2.0**100
NEVER = -1e30
VMEM_LIMIT = 60 * 1024 * 1024
PROJECT_LIMIT = 16 * 1024 * 1024


def table_kernel(planes, plane_size, group, frames_here, place_ref, ends_ref, table_ref):
    block = pl.program_id(0)
    plane, place = place_ref[0], place_ref[1]
    assert planes in (1, 4)
    plane_frames = plane_size * frames_here
    key_frames = group * frames_here
    query_frames = planes * frames_here
    width = table_ref.shape[2]
    tiles = ends_ref.shape[1]
    step = 2 * UNROLL

    def bits(size):
        assert size & (size - 1) == 0
        return size.bit_length() - 1

    def iota(shape, axis):
        return lax.broadcasted_iota(jnp.int32, shape, axis)

    candidates = []
    for side in range(2):
        for tile in range(tiles):
            pair = [ends_ref[end, tile : tile + 1] ^ (plane << bits(plane_frames)) for end in (side, 1 - side)]
            candidates.append((pair[0], pair[1], None))
    lane = iota((1, LANES), 1)
    chunk = lane >> bits(frames_here)
    mine = (
        ((((chunk & 1) << 1) + (((chunk >> 1) ^ chunk) & 1)) << bits(plane_frames))
        + (place << bits(frames_here))
        + (lane & (frames_here - 1))
    )
    candidates.append((mine, mine, lane < query_frames))

    lives, queries, keys, hits = [], [], [], []
    for asked, key, valid in candidates:
        live = (key >> bits(key_frames) == block) & (
            (asked >> bits(frames_here)) & (plane_size - 1) == place
        )
        if valid is not None:
            live = live & valid
        distance = asked >> bits(plane_frames)
        chunk = ((distance ^ (distance >> 1)) & 1) * 2 + (distance >> 1)
        query = (chunk << bits(frames_here)) + (asked & (frames_here - 1))
        query = jnp.where(live, query, query_frames)
        lives.append(live)
        queries.append(query)
        keys.append(key & (key_frames - 1))
        hits.append(jnp.where(query == iota((query_frames, LANES), 0), 1.0, 0.0))
    stacked = jnp.concatenate(hits, axis=0).astype(jnp.bfloat16)

    def product(left, right):
        return jnp.dot(left.astype(jnp.bfloat16), right.astype(jnp.bfloat16), preferred_element_type=jnp.float32)

    def ones_where(condition):
        return jnp.where(condition, 1.0, 0.0)

    square = (LANES, LANES)
    earlier = product(stacked, ones_where(iota(square, 0) < iota(square, 1)))
    every = product(stacked, jnp.ones(square, jnp.float32))
    before = [jnp.zeros((query_frames, LANES), jnp.float32)]
    for tile in range(len(hits)):
        before.append(before[-1] + every[tile * query_frames : (tile + 1) * query_frames])
    used = 2.0 * jnp.floor((before[-1] + 1.0) * 0.5)
    square = (query_frames, query_frames)
    row, column = iota(square, 0), iota(square, 1)
    row_chunk, column_chunk = row >> bits(frames_here), column >> bits(frames_here)
    inside = product(ones_where((row_chunk == column_chunk) & (column < row)), used)
    whole = product(ones_where(row_chunk == column_chunk), used)
    steps = jnp.floor((whole + (step - 1.0)) * (1.0 / step))
    leads = column & (frames_here - 1) == 0
    chunk_start = product(ones_where((column_chunk < row_chunk) & leads), steps)
    start = inside + step * chunk_start

    frame = iota((query_frames, LANES), 0)
    at = iota((query_frames, LANES), 1)
    first = frame & (frames_here - 1) == 0
    starts = jnp.where(first & (at == frame >> bits(frames_here)), chunk_start, 0.0)
    starts = starts + jnp.where(first & (at == planes), steps, 0.0)
    starts = jnp.sum(starts, axis=0, keepdims=True).astype(jnp.int32)

    placed, values = [], []
    for tile, hit in enumerate(hits):
        rank = earlier[tile * query_frames : (tile + 1) * query_frames] + before[tile] + start
        slot = jnp.sum(hit * rank, axis=0, keepdims=True).astype(jnp.int32)
        slot = jnp.where(lives[tile], slot, -1)
        placed.append(ones_where(slot == iota((width, LANES), 0)).astype(jnp.bfloat16))
        kind = iota((8, LANES), 0)
        value = jnp.where(kind == 0, queries[tile], jnp.where(kind == 1, keys[tile], 1))
        values.append(value.astype(jnp.float32).astype(jnp.bfloat16))
    codes = lax.dot_general(
        jnp.concatenate(values, axis=1),
        jnp.concatenate(placed, axis=1),
        (((1,), (1,)), ((), ())),
        preferred_element_type=jnp.float32,
    ).astype(jnp.int32)
    code = jnp.where(codes[2:3] > 0, (codes[0:1] << SHIFT) + codes[1:2], DEAD)
    starts = jnp.concatenate([starts] * (width // LANES), axis=1)
    table_ref[0] = jnp.where(iota((2, width), 0) == 0, code, starts)


def attend_table(pair_list, planes, plane_size, group, frames_here, places):
    peers = planes * plane_size
    rows = pair_list.shape[0]
    blocks = peers // group
    number = 2 * planes * group * (rows // peers // peers) + frames_here
    most = number + planes * frames_here + planes * (2 * UNROLL - 2)
    width = (most + LANES - 1) // LANES * LANES
    ends = pair_list.T.reshape(2, rows // LANES, LANES)
    return pl.pallas_call(
        functools.partial(table_kernel, planes, plane_size, group, frames_here),
        grid=(blocks,),
        in_specs=[
            pl.BlockSpec(memory_space=pltpu.SMEM),
            pl.BlockSpec(ends.shape, lambda block: (0, 0, 0)),
        ],
        out_specs=pl.BlockSpec((1, 2, width), lambda block: (block, 0, 0)),
        out_shape=jax.ShapeDtypeStruct((blocks, 2, width), jnp.int32),
        compiler_params=pltpu.CompilerParams(vmem_limit_bytes=VMEM_LIMIT),
    )(places, ends)


def attend_kernel(
    begin, number, chunks, sources, states, ends, table_ref, place_ref, order_ref, *refs
):
    del order_ref
    query_refs, refs = refs[: len(chunks)], refs[len(chunks) :]
    pair_refs = []
    for parts in sources:
        pair_refs.append(refs[:parts])
        refs = refs[parts:]
    state_refs, refs = refs[: 2 * states], refs[2 * states :]
    done_ref, refs = refs[0], refs[1:]
    done_ref[...] = jnp.zeros_like(done_ref)
    outs = len(chunks) if ends else 2
    out_refs, refs = refs[:outs], refs[outs:]
    sum_ref, total_ref, pair_ref, wide_ref, query_ref, score_ref, arrived, left = refs[:8]
    frames_here = query_refs[0].shape[0]
    group = pair_ref.shape[2]
    per_source = max(pair_refs[0][0].shape[0] // group, 1)
    first_frame = chunks[0] * frames_here
    query_frames = len(chunks) * frames_here
    held_from = 0 if ends else begin

    def copies(block, slot, source):
        refs_here = pair_refs[source]
        devices = pl.ds(block % per_source * group, group)
        return [
            pltpu.make_async_copy(
                refs_here[0].at[devices, kind], pair_ref.at[slot, kind], arrived.at[2 * slot + kind]
            )
            for kind in range(2)
        ]

    def fetch(block, slot):
        for source in range(len(sources)):

            @pl.when((block - held_from) // per_source == source)
            def _():
                for copy in copies(block, slot, source):
                    copy.start()

    def over_blocks(first_block, turns, step, ahead=None, before=None, behind=None):
        def visit(turn, carry):
            block = first_block + turn

            @pl.when(turn + 1 < turns)
            def _():
                fetch(block + 1, (turn + 1) % 2)

            def wait_for(kind):
                here = pair_ref.at[turn % 2, kind]
                pltpu.make_async_copy(here, here, arrived.at[2 * (turn % 2) + kind]).wait()

            wait_for(0)

            def units_of(index):
                first = index * 2 * UNROLL
                codes = [table_ref[block, 0, first + member] for member in range(2 * UNROLL)]
                return [codes[2 * unit : 2 * unit + 2] for unit in range(UNROLL)]

            def several(index, inner):
                step(turn % 2, units_of(index), units_of(index + 1) if ahead else None)
                return inner

            for index, chunk in enumerate(chunks):
                if before:
                    before(index)
                begins = table_ref[block, 1, chunk]
                if ahead:
                    ahead(turn % 2, units_of(begins))
                if index == 0:
                    wait_for(1)
                lax.fori_loop(begins, table_ref[block, 1, chunk + 1], several, 0)
                if behind:
                    behind(index)
            return carry

        if turns == 1:
            visit(0, 0)
        else:
            lax.fori_loop(0, turns, visit, 0)

    def frames_at(slot, unit):
        keys = []
        for code in unit:
            key_frame = code & ((1 << SHIFT) - 1)
            keys.append((slot, key_frame // frames_here, key_frame % frames_here))
        here = (unit[0] >> SHIFT) - first_frame
        return jnp.where((here >= 0) & (here < query_frames), here, 0), keys

    def scores_of(slot, unit):
        query_frame, keys = frames_at(slot, unit)
        held = jnp.concatenate([pair_ref[slot, 0, device, frame] for slot, device, frame in keys], axis=0)
        return lax.dot_general(
            wide_ref[query_frame], held, (((1,), (1,)), ((), ())), preferred_element_type=jnp.float32
        )

    def bias_of(unit):
        lane = lax.broadcasted_iota(jnp.int32, (1, PACKED), 1)
        bias = [jnp.where(code < DEAD, 0.0, NEVER) for code in unit]
        return jnp.where(lane < TOKF, bias[0], bias[1])

    def sums_of(keys, weights):
        held = jnp.concatenate([pair_ref[slot, 1, device, frame] for slot, device, frame in keys], axis=0)
        return by_head(
            jnp.dot(weights.astype(jnp.bfloat16), held, preferred_element_type=jnp.float32)
        )

    def by_head(both):
        lane = lax.broadcasted_iota(jnp.int32, (TOKF, LANES), 1)
        return jnp.where(lane < HDIM, both[:TOKF], both[TOKF:])

    def totals_of(weights):
        folded = weights[:, :LANES] + weights[:, LANES : 2 * LANES] + weights[:, 2 * LANES :]
        return by_head(folded + pltpu.roll(folded, HDIM, 1))

    def look_ahead(slot, units):
        for place, unit in enumerate(units):
            score_ref[place] = scores_of(slot, unit)

    def plain(slot, units, following):
        results = []
        for place, unit in enumerate(units):
            query_frame, keys = frames_at(slot, unit)
            weights = jnp.exp(score_ref[place] + bias_of(unit))
            score_ref[place] = scores_of(slot, following[place])
            results.append((query_frame, sums_of(keys, weights), totals_of(weights)))
        for query_frame, summed, total in results:
            sum_ref[query_frame] += summed
            total_ref[query_frame] += total

    asked = [
        pltpu.make_async_copy(ref, query_ref.at[index], left.at[index])
        for index, ref in enumerate(query_refs)
    ]
    for copy in asked:
        copy.start()
    fetch(begin, 0)
    frames_of = [pl.ds(index * frames_here, frames_here) for index in range(len(chunks))]
    taken, put = [], []
    for piece in range(states):
        old_refs = state_refs[2 * piece : 2 * piece + 2]
        pieces_chunks = old_refs[0].shape[0] // frames_here
        for index in range(pieces_chunks):
            if len(taken) == len(chunks):
                break
            begin_chunk = chunks[0] if states == 1 and pieces_chunks > len(chunks) else 0
            source = pl.ds((begin_chunk + index) * frames_here, frames_here)
            place = len(taken)
            taken.append(
                [
                    pltpu.make_async_copy(
                        old_ref.at[source], new_ref.at[frames_of[place]], arrived.at[4 + place]
                    )
                    for old_ref, new_ref in zip(old_refs, (sum_ref, total_ref))
                ]
            )
    for copies_here in taken:
        for copy in copies_here:
            copy.start()

    def widen(index):
        asked[index].wait()

        def one(frame, carry):
            rows = query_ref[index, frame] * jnp.asarray(HDIM**-0.5, wide_ref.dtype)
            first = lax.broadcasted_iota(jnp.int32, rows.shape, 1) < HDIM
            zeros = jnp.zeros_like(rows)
            wide_ref[index * frames_here + frame, :TOKF] = jnp.where(first, rows, zeros)
            wide_ref[index * frames_here + frame, TOKF:] = jnp.where(first, zeros, rows)
            return carry

        lax.fori_loop(0, frames_here, one, 0, unroll=4)

    def clear(frame, carry):
        sum_ref[frame] = jnp.zeros(sum_ref.shape[1:], sum_ref.dtype)
        total_ref[frame] = jnp.zeros(total_ref.shape[1:], total_ref.dtype)
        return carry

    for index in range(len(chunks)):
        widen(index)
    if not states:
        lax.fori_loop(0, query_frames, clear, 0, unroll=4)

    def enter(index):
        if states:
            for ref in (sum_ref, total_ref):
                part = ref.at[frames_of[index]]
                pltpu.make_async_copy(part, part, arrived.at[4 + index]).wait()

    def leave(index):
        if not ends:
            for ref, out in zip((sum_ref, total_ref), out_refs):
                copy = pltpu.make_async_copy(
                    ref.at[frames_of[index]], out.at[frames_of[index]], left.at[index]
                )
                copy.start()
                put.append(copy)

    if number == 1:
        over_blocks(begin, number, plain, look_ahead, enter, leave)
    else:
        for index in range(len(chunks)):
            enter(index)
        over_blocks(begin, number, plain, look_ahead)
        for index in range(len(chunks)):
            leave(index)
    for copy in put:
        copy.wait()
    if not ends:
        return
    whole_ref, top_ref = refs[8:]

    def gather_totals(frame, carry):
        total = total_ref[frame]
        square = (LANES, LANES)
        same = lax.broadcasted_iota(jnp.int32, square, 0) // HDIM == lax.broadcasted_iota(jnp.int32, square, 1) // HDIM
        ones = jnp.where(same, 1.0, 0.0).astype(jnp.bfloat16)
        high = total.astype(jnp.bfloat16)
        low = (total - high.astype(jnp.float32)).astype(jnp.bfloat16)
        whole_ref[frame] = jnp.dot(high, ones, preferred_element_type=jnp.float32) + jnp.dot(
            low, ones, preferred_element_type=jnp.float32
        )
        return carry

    lax.fori_loop(0, query_frames, gather_totals, 0, unroll=4)
    within = (jnp.min(whole_ref[...]) > LOW) & (jnp.max(whole_ref[...]) < HIGH)

    @pl.when(jnp.logical_not(within))
    def _():
        lax.fori_loop(0, query_frames, clear, 0)
        top_ref[...] = jnp.full_like(top_ref, 2 * NEVER)

        def shifted(slot, units, _):
            for unit in units:
                query_frame, keys = frames_at(slot, unit)
                scores = scores_of(slot, unit) + bias_of(unit)
                old = top_ref[query_frame]
                new = jnp.maximum(old, jnp.max(scores, axis=1, keepdims=True))
                keep = by_head(jnp.exp(old - new))
                weights = jnp.exp(scores - new[:, :1])
                sum_ref[query_frame] = sum_ref[query_frame] * keep + sums_of(keys, weights)
                total_ref[query_frame] = total_ref[query_frame] * keep + totals_of(weights)
                top_ref[query_frame] = new

        fetch(0, 0)
        over_blocks(0, len(sources) * per_source, shifted)
        lax.fori_loop(0, query_frames, gather_totals, 0)

    for index, out_ref in enumerate(out_refs):

        def finish(frame, carry):
            here = index * frames_here + frame
            out_ref[frame] = (sum_ref[here] / whole_ref[here]).astype(out_ref.dtype)
            return carry

        lax.fori_loop(0, frames_here, finish, 0, unroll=4)


def attend(queries, chunks, pairs, table, places, order, begin, number, group, state, ends):
    frames_here = queries[0].shape[0]
    shape = (len(chunks) * frames_here, TOKF, LANES)
    held = jax.ShapeDtypeStruct(shape, jnp.float32)
    whole = pl.BlockSpec(memory_space=pltpu.VMEM)
    scalars = pl.BlockSpec(memory_space=pltpu.SMEM)
    stays = pl.BlockSpec(memory_space=pltpu.HBM)
    room = pltpu.VMEM(shape, jnp.float32)
    wide = (shape[0], PACKED, LANES)
    common = [
        pltpu.VMEM((2, 2, group) + pairs[0][0].shape[2:], queries[0].dtype),
        pltpu.VMEM(wide, queries[0].dtype),
        pltpu.VMEM((len(chunks),) + queries[0].shape, queries[0].dtype),
        pltpu.VMEM((UNROLL, PACKED, PACKED), jnp.float32),
        pltpu.SemaphoreType.DMA((4 + len(chunks),)),
        pltpu.SemaphoreType.DMA((len(chunks),)),
    ]
    listed = [array for plane in pairs for array in plane] + [array for pair in state for array in pair]
    return pl.pallas_call(
        functools.partial(
            attend_kernel,
            begin,
            number,
            tuple(chunks),
            tuple(len(plane) for plane in pairs),
            len(state),
            ends,
        ),
        in_specs=[scalars, scalars] + [stays] * (1 + len(queries) + len(listed)),
        out_specs=[whole] + ([whole] * len(chunks) if ends else [stays, stays]),
        out_shape=[jax.ShapeDtypeStruct(order.shape, order.dtype)]
        + (
            [jax.ShapeDtypeStruct(query.shape, query.dtype) for query in queries]
            if ends
            else [held, held]
        ),
        scratch_shapes=[room] * 2
        + common
        + ([room, pltpu.VMEM(wide, jnp.float32)] if ends else []),
        compiler_params=pltpu.CompilerParams(vmem_limit_bytes=VMEM_LIMIT),
        cost_estimate=pl.CostEstimate(flops=1, bytes_accessed=1, transcendentals=0),
    )(table, places, order, *queries, *listed)


def project_kernel(parts, place_ref, *refs):
    del place_ref
    row_refs, weight_refs, refs = refs[:parts], refs[parts : 2 * parts], refs[2 * parts :]
    out_ref = refs[-1]
    total = jnp.dot(
        jnp.concatenate([ref[...] for ref in row_refs], axis=1),
        jnp.concatenate([ref[...] for ref in weight_refs], axis=0),
        preferred_element_type=jnp.float32,
    )
    if len(refs) > 1:
        total = total + refs[0][...]
    out_ref[...] = total.astype(out_ref.dtype)


def project(parts, near, far, places, total, ends):
    rows = parts[0][2].shape[0]
    tile = rows // 4 if rows % 64 == 0 else rows
    columns = far.shape[1]

    def weight_spec(other, distance):
        def place(row, at):
            return (at[0] ^ distance, 0 if other else at[2])

        return pl.BlockSpec((LANES, columns), place)

    kept = pl.BlockSpec((tile, columns), lambda row, at: (row, 0))
    return pl.pallas_call(
        functools.partial(project_kernel, len(parts)),
        grid_spec=pltpu.PrefetchScalarGridSpec(
            num_scalar_prefetch=1,
            grid=(rows // tile,),
            in_specs=[pl.BlockSpec((tile, LANES), lambda row, at: (row, 0)) for _ in parts]
            + [weight_spec(other, distance) for other, distance, _ in parts]
            + ([] if total is None else [kept]),
            out_specs=kept,
        ),
        out_shape=jax.ShapeDtypeStruct((rows, columns), near.dtype if ends else jnp.float32),
        compiler_params=pltpu.CompilerParams(vmem_limit_bytes=PROJECT_LIMIT),
        cost_estimate=pl.CostEstimate(flops=1, bytes_accessed=1, transcendentals=0),
    )(
        places,
        *(part for _, _, part in parts),
        *(far if other else near for other, _, _ in parts),
        *(() if total is None else (total,)),
    )


def spread(queries, pairs, far, table, places, swap, across, gather, plane_size):
    chunk_order = [0, 3, 1, 2]
    barrier = lax.optimization_barrier
    order = jnp.zeros((8, LANES), jnp.int32)

    def run(distances, plane, keyed, state, ends=False, number=1):
        return attend(
            [queries[distance] for distance in distances],
            [chunk_order.index(distance) for distance in distances],
            keyed if ends else keyed[plane : plane + number],
            table,
            places,
            order,
            plane,
            number,
            plane_size,
            state,
            ends,
        )

    def gathered(distance):
        return [gather(pairs[distance], plane_size)]

    keyed = [gathered(0), None, None, None]
    pairs[1], queries[3] = swap(pairs[1], 1), swap(queries[3], 3)
    pairs[1], queries[3], queries[1], pairs[3], table, order = barrier(
        (pairs[1], queries[3], queries[1], pairs[3], table, order)
    )
    keyed[1] = gathered(1)
    pairs[3], queries[1] = swap(pairs[3], 3), swap(queries[1], 1)
    order, *early = run([0, 3], 0, keyed, [])
    queries[1], pairs[3], pairs[2], order = barrier((queries[1], pairs[3], pairs[2], order))
    keyed[3] = gathered(3)
    pairs[2] = swap(pairs[2], 2)
    order, *late = run([1], 0, keyed, [])
    order, *state = run([0, 3, 1], 1, keyed, [early, late])
    pairs[2], queries[2], far, order = barrier((pairs[2], queries[2], far, order))
    keyed[2] = gathered(2)
    queries[2] = swap(queries[2], 2)
    order, *state = run([0, 3, 1], 3, keyed, [state])
    queries[2], far, order = barrier((queries[2], far, order))
    far = across(far)
    order, *last = run([2], 0, keyed, [], number=2)
    merged, others = [None] * 4, [None] * 4

    def rows_of(out):
        return out.reshape(-1, LANES)

    order, *outs = run([0, 3, 1], 2, keyed, [state], True)
    merged[0], out, near_out, order = barrier(tuple(map(rows_of, outs)) + (order,))
    merged[3], merged[1], others[0] = swap(out, 3), swap(near_out, 1), across(merged[0])
    order, out = run([2], 2, keyed, [last], True, 2)
    out, merged[3], merged[1], others[0], far = barrier(
        (rows_of(out), merged[3], merged[1], others[0], far)
    )
    merged[2], others[1], others[3] = swap(out, 2), across(merged[1]), across(merged[3])
    others[2] = across(merged[2])
    return merged, others, far


def body(query_states, key_states, value_states, pair_list, out_weight):
    peers = lax.axis_size("frames")
    my_index = lax.axis_index("frames")
    rows, columns = query_states.shape
    frames_here = rows // TOKF
    planes = columns // LANES
    plane_size = peers // planes
    group = min(plane_size, GROUP)
    plane, place = my_index // plane_size, my_index % plane_size
    side = lax.axis_index("heads")
    places = jnp.stack([plane, place, side]).astype(jnp.int32)
    table = attend_table(pair_list, planes, plane_size, group, frames_here, places)
    per_plane = plane_size // group

    def swap(array, distance, axis=plane_size):
        if distance == 0:
            return array
        return lax.ppermute(
            array, "frames", [(index, index ^ (distance * axis)) for index in range(peers)]
        )

    def gather(array, size):
        members = [list(range(start, start + size)) for start in range(0, peers, size)]
        return lax.all_gather(array, "frames", axis_index_groups=members)

    def across(array):
        return lax.ppermute(array, "heads", [(0, 1), (1, 0)])

    def columns_of(array, distance):
        chosen = lax.dynamic_slice_in_dim(array, (plane ^ distance) * LANES, LANES, 1)
        return chosen.reshape(frames_here, TOKF, LANES)

    queries = [columns_of(query_states, distance) for distance in range(planes)]
    pairs = [
        jnp.stack([columns_of(key_states, distance), columns_of(value_states, distance)])
        for distance in range(planes)
    ]
    two = lax.axis_size("heads") == 2
    far = lax.dynamic_slice_in_dim(out_weight, (1 - side) * columns, columns, 1)
    if planes == 1:
        keyed = [[gather(pairs[0], plane_size)]]
        order = jnp.zeros((8, LANES), jnp.int32)
        _, out = attend(
            queries, [0], keyed, table, places, order, 0, per_plane, group, [], True
        )
        out = out.reshape(rows, LANES)
        if not two:
            term = jnp.dot(out, out_weight, preferred_element_type=jnp.float32)
            return lax.psum_scatter(
                term.astype(out.dtype), "heads", scatter_dimension=1, tiled=True
            )
        parts = [(False, 0, out), (True, 0, across(out))]
        return project(parts, out_weight, across(far), places, None, True)
    assert two
    merged, others, far = spread(
        queries, pairs, far, table, places, swap, across, gather, plane_size
    )
    ready = [(False, distance, merged[distance]) for distance in range(planes)]
    ready += [(True, distance, others[distance]) for distance in (0, 1, 3)]
    total = project(ready, out_weight, far, places, None, False)
    return project([(True, 2, others[2])], out_weight, far, places, total, True)


def solution(mesh):
    placed = (
        P("frames", "heads"),
        P("frames", "heads"),
        P("frames", "heads"),
        P(),
        P("heads", None),
    )
    return jax.shard_map(
        body, mesh=mesh, in_specs=placed, out_specs=P("frames", "heads"), check_vma=False
    )
```
